512 devices in a mesh: ax: 32 (over x, z), tr: 16 (over y, core).
Axes of the slice: x: 4, y: 8, z: 8, core: 2. Of those that a mesh axis runs over, the one named last changes fastest.
Arguments:
- solid_start: bfloat16 [64, 1024, 4096], P(None, 'ax', 'tr'), may hold values from -80 to 80
- inlet: float32 [64, 4096], P(None, 'tr'), may hold values from -4 to 4
- ntu: float32 [1024, 4096], P('ax', 'tr'), may hold values from 0 to 1
- solid_rate: float32 [1024, 4096], P('ax', 'tr'), may hold values from 0.2 to 0.8
Outputs:
- basis: float32 [64, 2, 1024, 4096], P(None, None, 'ax', 'tr')
- factor: float32 [64, 64], replicated
The draws below stay inside these ranges and needn't reach their ends.
All inputs are finite; a program needn't handle non-finite values.
Results may differ from the reference program's by a relative error of at most 0.0003.
Values sent between devices are 32-bit elements; how exact they have to be, the bound alone decides.
A program may use at most 128 MiB of HBM per device.

```python
import math
import jax
import jax.numpy as jnp
from jax import lax

NS = 64
STEPS = 2
AXIAL_COUNT = 1024
TRANSVERSE_COUNT = 4096
ROWS = 8388608


def draw_ntu(key, part):
    key = jax.random.fold_in(key, 11)
    key_parent, key_roughness, key_plane_draw, key_spike = jax.random.split(key, 4)
    upper_log = math.log(0.1)
    base = jnp.exp(jax.random.uniform(key_parent, (1, TRANSVERSE_COUNT), jnp.float32, math.log(0.05 / AXIAL_COUNT), upper_log))
    rough = jax.random.uniform(key_roughness, (AXIAL_COUNT, TRANSVERSE_COUNT), jnp.float32, 0.5, 1.5)
    spike_plane_list = jax.random.randint(key_plane_draw, (2,), 0, AXIAL_COUNT)
    axial_plane_index = jnp.arange(AXIAL_COUNT)[:, None]
    spike_active = ((axial_plane_index == spike_plane_list[0]) | (axial_plane_index == spike_plane_list[1])).astype(jnp.float32)
    spike_magnitude = jax.random.uniform(key_spike, (1, TRANSVERSE_COUNT), jnp.float32, 0.25, 0.7)
    return base * rough + spike_active * spike_magnitude


def draw_solid_start(key, part):
    key = jax.random.fold_in(key, 12)
    key_noise = jax.random.fold_in(key, 0)
    key_rows = jax.random.fold_in(key, 2)
    key_columns = jax.random.fold_in(key, 3)
    plane_ramp = 0.6 + 1.2 * (jnp.arange(AXIAL_COUNT, dtype=jnp.float32) / AXIAL_COUNT)[None, :, None]
    noise = jnp.clip(jax.random.normal(key_noise, (NS, AXIAL_COUNT, TRANSVERSE_COUNT), jnp.float32), -4.0, 4.0)
    row_scale = jnp.exp(jax.random.uniform(key_rows, (1, AXIAL_COUNT, TRANSVERSE_COUNT), jnp.float32, math.log(0.3), math.log(3.0)))
    column_scale = jnp.exp(jax.random.uniform(key_columns, (NS, 1, 1), jnp.float32, 0.0, math.log(3.0)))
    return (noise * row_scale * plane_ramp * column_scale).astype(jnp.bfloat16)


def block_scale(rng, extent, cuts, smallest, high):
    def one(position, shards_of):
        steps = jax.random.uniform(jax.random.fold_in(jax.random.fold_in(rng, 6), position), (shards_of,), jnp.float32, smallest / len(cuts), high / len(cuts))
        return jnp.repeat(jnp.exp(steps), extent[position] // shards_of).reshape((-1,) + (1,) * (len(extent) - position - 1))

    level = one(*cuts[0])
    for cut in cuts[1:]:
        level = level * one(*cut)
    return level


def centred(rng, extent, width, most, cuts=(), held_as=jnp.bfloat16):
    entries = width * jax.random.normal(rng, extent, jnp.float32)
    if cuts:
        entries = entries * block_scale(rng, extent, cuts, -0.22, 0.18)
    return jnp.clip(entries, -most, most).astype(held_as)


def setup_inputs(seed: int = 0) -> dict:
    splits = jax.random.split(jax.random.key(seed), 5)
    solid_start = draw_solid_start(jax.random.fold_in(splits[4], 71), 0)
    inlet = centred(splits[1], (NS, TRANSVERSE_COUNT), 1.0, 4.0, ((1, 16),), jnp.float32)
    ntu = draw_ntu(jax.random.fold_in(splits[4], 71), 0)
    solid_rate = jnp.clip(0.2 + 0.6 * jax.random.uniform(splits[3], (AXIAL_COUNT, TRANSVERSE_COUNT), jnp.float32) ** block_scale(splits[3], (AXIAL_COUNT, TRANSVERSE_COUNT), ((0, 32), (1, 16)), -0.2, 0.2), 0.2, 0.8)
    return {"solid_start": solid_start, "inlet": inlet, "ntu": ntu, "solid_rate": solid_rate}


def reference(solid_start, inlet, ntu, solid_rate):
    carry_coef = 1.0 / (1.0 + ntu)
    source_coef = ntu / (1.0 + ntu)
    solid_planes = jnp.transpose(solid_start.astype(jnp.float32), (1, 0, 2))

    def march(carried, layer_data):
        coef_plane, source_plane, solid_plane = layer_data
        carried = coef_plane[None, :] * carried + source_plane[None, :] * solid_plane
        return (carried, carried)
    fluid_planes = solid_planes
    for repeat in range(STEPS):
        ignored, fluid_planes = lax.scan(march, inlet, (carry_coef, source_coef, solid_planes))
        solid_planes = solid_planes + solid_rate[:, None, :] * (fluid_planes - solid_planes)
    gram_matrix = jnp.einsum('zns,zms->nm', fluid_planes, fluid_planes, precision=lax.Precision.HIGHEST)
    gram_matrix = gram_matrix + jnp.einsum('zns,zms->nm', solid_planes, solid_planes, precision=lax.Precision.HIGHEST)
    lower_factor = jnp.linalg.cholesky(gram_matrix)
    root_rows = jnp.sqrt(jnp.float32(ROWS))
    inverse = lax.linalg.triangular_solve(lower_factor, jnp.eye(NS, dtype=jnp.float32), left_side=True, lower=True)
    fluid_basis = jnp.einsum('nm,zms->nzs', inverse, fluid_planes, precision=lax.Precision.HIGHEST)
    solid_basis = jnp.einsum('nm,zms->nzs', inverse, solid_planes, precision=lax.Precision.HIGHEST)
    basis = jnp.stack([fluid_basis, solid_basis], axis=1) * root_rows
    factor = lower_factor.T / root_rows
    return (basis, factor)
```

```python
import functools

import jax
import jax.numpy as jnp
from jax import lax
from jax.experimental import pallas as pl
from jax.experimental.pallas import tpu as pltpu
from jax.sharding import PartitionSpec as P

MESH = pl.DeviceIdType.MESH
F32 = jnp.float32
BF16 = jnp.bfloat16
NS = 64
NZ = 32
NT = 256
LZ, LX, LY = 8, 4, 8
SLICE = NT // LZ


def split(value):
    high = value.astype(BF16)
    low = (value - high.astype(F32)).astype(BF16)
    return high, low


def place():
    ax, tr = lax.axis_index("ax"), lax.axis_index("tr")
    return ax // LZ, lax.rem(ax, LZ), tr // 2, lax.rem(tr, 2)


def device(x, z, y, c):
    return {"ax": x * LZ + z, "tr": y * 2 + c}


def ring(count, body):
    def step(i, carry):
        body(i)
        return carry

    lax.fori_loop(1, count, step, 0)


def await_bytes(ref, sem):
    pltpu.make_async_copy(ref, ref, sem).wait()


def sweep_kernel(
    solid, inlet, ntu, rate,
    gram_out, snap_out,
    xb, ntu_v, rate_v, inlet_v, xs, coef, snap0, ends, snap,
    send_c, send_bu, send_x, send_e, send_g, send_h,
    recv_c, recv_bu, recv_x, recv_e, recv_g, recv_h,
    coef_t, inlet_t, total, load_sem, out_sem, ssem, rsem,
):
    x, z, y, c = place()
    xc = x * 2 + c

    loads = [
        pltpu.make_async_copy(src, dst, load_sem.at[i])
        for i, (src, dst) in enumerate(
            [(ntu, ntu_v), (rate, rate_v), (solid, xb), (inlet, inlet_v)]
        )
    ]
    for load in loads:
        load.start()

    def peer_z(i):
        return lax.rem(z + i, LZ)

    def peer_y(i):
        return lax.rem(y + i, LY)

    def peer_xc(i):
        return lax.rem(xc + i, 2 * LX)

    def dev_z(i):
        return device(x, peer_z(i), y, c)

    def dev_y(i):
        return device(x, z, peer_y(i), c)

    def dev_xc(i):
        p = peer_xc(i)
        return device(p // 2, z, y, lax.rem(p, 2))

    barrier = pltpu.get_barrier_semaphore()
    for count, dev in ((LZ, dev_z), (2 * LX, dev_xc), (LY, dev_y)):
        ring(count, lambda i, dev=dev: pl.semaphore_signal(
            barrier, inc=1, device_id=dev(i), device_id_type=MESH))

    loads[0].wait()
    loads[1].wait()
    n_all = ntu_v[...]
    r_all = rate_v[...]
    a_all = 1.0 / (1.0 + n_all)
    s_all = n_all / (1.0 + n_all)
    coef[0] = a_all.reshape(NZ // 8, 8, NT)
    coef[1] = s_all.reshape(NZ // 8, 8, NT)
    coef[6] = r_all.reshape(NZ // 8, 8, NT)
    sr_all = s_all * r_all
    p = jnp.ones((1, NT), F32)
    q = jnp.zeros((1, NT), F32)
    for k in range(NZ):
        a = a_all[k : k + 1]
        p = a * p
        q = a * q + sr_all[k : k + 1] * p
        coef[2, k // 8, k % 8 : k % 8 + 1, :] = p
        coef[3, k // 8, k % 8 : k % 8 + 1, :] = q
    p_all = coef[2].reshape(NZ, NT)
    q_all = coef[3].reshape(NZ, NT)
    bw = r_all * p_all
    aw = (1.0 - r_all) * bw + r_all * q_all
    coef[4] = bw.reshape(NZ // 8, 8, NT)
    coef[5] = aw.reshape(NZ // 8, 8, NT)
    both = lambda u: jnp.sum(u, axis=0, keepdims=True)
    rows = jnp.concatenate(
        [
            p, q,
            0.5 * both(q_all * q_all + aw * aw),
            both(q_all * p_all + aw * bw),
            0.5 * both(p_all * p_all + bw * bw),
            jnp.zeros((3, NT), F32),
        ],
        axis=0,
    )
    send_c[0] = rows[:, :128]
    send_c[1] = rows[:, 128:]

    loads[2].wait()
    chunk = 16

    def widen(i, carry):
        part = xb[pl.ds(i * 8, 8)].astype(F32)
        for h in range(2):
            xs[h, pl.ds(i * 8 * NZ, 8 * NZ), :] = part[:, :, h * 128 : h * 128 + 128].reshape(8 * NZ, 128)
        return carry

    lax.fori_loop(0, NS // 8, widen, 0)

    def sweep_chunk(ci, carry):
        n0 = ci * chunk

        def plane(kg, i, state):
            new = []
            k = kg * 8 + i
            for h in range(2):
                f1, f2, u1, u2 = state[h]
                lanes = pl.ds(h * 128, 128)
                one = lambda m: jnp.broadcast_to(coef[m, kg, i : i + 1, lanes], (chunk, 128))
                a, s, pp, qq, bb, aa, r = (one(m) for m in range(7))
                v = xs[h, pl.ds(n0 * NZ + k, chunk, stride=NZ), :]
                f1 = a * f1 + s * v
                v = v + r * (f1 - v)
                f2 = a * f2 + s * v
                w = v + r * (f2 - v)
                snap0[k, pl.ds(n0, chunk), lanes] = f2
                snap0[NZ + k, pl.ds(n0, chunk), lanes] = w
                u1 = u1 + (qq * f2 + aa * w)
                u2 = u2 + (pp * f2 + bb * w)
                new.append((f1, f2, u1, u2))
            return tuple(new)

        def planes(kg, state):
            for i in range(8):
                state = plane(kg, i, state)
            return state

        zero = jnp.zeros((chunk, 128), F32)
        state = lax.fori_loop(0, NZ // 8, planes, ((zero,) * 4,) * 2)
        for h in range(2):
            for m in range(4):
                ends[m, pl.ds(n0, chunk), h * 128 : h * 128 + 128] = state[h][m]
        return carry

    lax.fori_loop(0, NS // chunk, sweep_chunk, 0)
    for m in range(2):
        flat = jnp.concatenate([ends[2 * m], ends[2 * m + 1]], axis=0)
        send_bu[m] = flat.T.reshape(LZ, SLICE, 128)

    pl.semaphore_wait(barrier, (LZ - 1) + (2 * LX - 1) + (LY - 1))

    ring(LZ, lambda i: pltpu.make_async_remote_copy(
        send_c.at[peer_z(i) // 4], recv_c.at[z], ssem.at[0], rsem.at[0],
        device_id=dev_z(i), device_id_type=MESH).start())
    for m in range(2):
        ring(LZ, lambda i: pltpu.make_async_remote_copy(
            send_bu.at[m, peer_z(i)], recv_bu.at[m, z], ssem.at[1 + m], rsem.at[1 + m],
            device_id=dev_z(i), device_id_type=MESH).start())
    recv_c[z] = send_c[z // 4]
    recv_bu[0, z] = send_bu[0, z]
    recv_bu[1, z] = send_bu[1, z]

    loads[3].wait()
    inl = inlet_v[...]
    inlet_t[...] = jnp.concatenate([inl, inl], axis=0).T.reshape(LZ, SLICE, 128)

    def inner(k, acc):
        high, low = split(snap0[k])
        rowsb = jnp.concatenate([high, low], axis=0)
        return acc + lax.dot_general(rowsb, rowsb, (((1,), (1,)), ((), ())), preferred_element_type=F32)

    acc = lax.fori_loop(0, 2 * NZ, inner, jnp.zeros((2 * NS, 2 * NS), F32), unroll=4)
    gram0 = (acc[:NS, :NS] + acc[NS:, NS:]) + (acc[:NS, NS:] + acc[NS:, :NS])

    await_bytes(recv_c.at[pl.ds(0, LZ - 1)], rsem.at[0])
    coef_t[...] = recv_c[...].reshape(LZ * 8, 128).T
    ct = coef_t[pl.ds(pl.multiple_of(lax.rem(z, 4) * SLICE, SLICE), SLICE), :]
    lane = lax.broadcasted_iota(jnp.int32, (SLICE, 128), 1)
    second = lane >= NS
    wide = lambda k, m: jnp.broadcast_to(ct[:, k * 8 + m : k * 8 + m + 1], (SLICE, 128))
    turn = lambda u: pltpu.roll(u, NS, 1)
    aks = [wide(k, 0) for k in range(LZ)]
    cks = [wide(k, 1) for k in range(LZ)]
    c2s = [jnp.where(second, ck, 0.0) for ck in cks]
    await_bytes(recv_bu.at[0, pl.ds(0, LZ - 1)], rsem.at[1])
    bks = [recv_bu[0, k] for k in range(LZ)]
    bds = [jnp.where(second, turn(b), b) for b in bks]
    full, dup, at, ctot = bks[0], bds[0], aks[0], cks[0]
    for k in range(1, LZ):
        full, dup = aks[k] * full + c2s[k] * dup + bks[k], aks[k] * dup + bds[k]
        at, ctot = aks[k] * at, aks[k] * ctot + cks[k] * at
    send_x[0] = full
    send_x[1] = jnp.where(second, ctot, at)

    def send_line(i):
        px = lax.rem(x + i, LX)
        pltpu.make_async_remote_copy(
            send_x, recv_x.at[x], ssem.at[3], rsem.at[3],
            device_id=device(px, z, y, c), device_id_type=MESH).start()

    ring(LX, send_line)
    recv_x[x] = send_x[...]
    await_bytes(recv_x.at[pl.ds(0, LX - 1)], rsem.at[3])
    e = inlet_t[z]
    d = e
    for k in range(LX - 1):
        f, cf = recv_x[k, 0], recv_x[k, 1]
        rolled = turn(cf)
        a = jnp.where(second, rolled, cf)
        c2 = jnp.where(second, cf, 0.0)
        fd = jnp.where(second, turn(f), f)
        e_new = a * e + c2 * d + f
        d_new = a * d + fd
        upstream = jnp.full((SLICE, 128), k, jnp.int32) < x
        e = jnp.where(upstream, e_new, e)
        d = jnp.where(upstream, d_new, d)
    for k in range(LZ):
        send_e[k] = e
        if k < LZ - 1:
            e, d = aks[k] * e + c2s[k] * d + bks[k], aks[k] * d + bds[k]
    ring(LZ, lambda i: pltpu.make_async_remote_copy(
        send_e.at[peer_z(i)], recv_e.at[z], ssem.at[4], rsem.at[4],
        device_id=dev_z(i), device_id_type=MESH).start())
    recv_e[z] = send_e[z]

    await_bytes(recv_bu.at[1, pl.ds(0, LZ - 1)], rsem.at[2])
    vs = []
    for k in range(LZ):
        ek = send_e[k]
        hk = jnp.where(second, wide(k, 4), wide(k, 2))
        abk = jnp.where(second, 0.0, wide(k, 3))
        vs.append(recv_bu[1, k] + hk * ek + abk * turn(ek))
    vh, vl = split(jnp.concatenate(vs, axis=0))
    eh, el = split(send_e[...].reshape(LZ * SLICE, 128))
    prod = lax.dot_general(
        jnp.concatenate([vh, vl], axis=1), jnp.concatenate([eh, el], axis=1),
        (((0,), (0,)), ((), ())), preferred_element_type=F32)
    prod = (prod[:128, :128] + prod[128:, 128:]) + (prod[:128, 128:] + prod[128:, :128])
    cross = prod[:NS, :NS] + prod[NS:, NS:]
    gram = gram0 + (cross + cross.T)
    send_g[...] = jnp.concatenate([gram[: NS // 2], gram[NS // 2 :]], axis=1)

    ring(2 * LX, lambda i: pltpu.make_async_remote_copy(
        send_g, recv_g.at[xc], ssem.at[5], rsem.at[5],
        device_id=dev_xc(i), device_id_type=MESH).start())
    recv_g[xc] = send_g[...]
    await_bytes(recv_g.at[pl.ds(0, 2 * LX - 1)], rsem.at[5])

    def add(parts):
        while len(parts) > 1:
            parts = [parts[i] + parts[i + 1] for i in range(0, len(parts), 2)]
        return parts[0]

    sums = add([recv_g[i] for i in range(2 * LX)])
    halves = [sums[:16], sums[16:]]
    for phase in range(2):
        for h in range(2):
            send_h[phase, h] = halves[h]
        for h in range(2):
            over_z = (h + phase) % 2 == 0
            dev, mine = (dev_z, z) if over_z else (dev_y, y)
            slot = 6 + 2 * phase + h
            ring(8, lambda i, dev=dev, mine=mine, slot=slot, h=h: pltpu.make_async_remote_copy(
                send_h.at[phase, h], recv_h.at[phase, h, mine], ssem.at[slot], rsem.at[slot],
                device_id=dev(i), device_id_type=MESH).start())
            recv_h[phase, h, mine] = halves[h]
        if phase == 0:
            await_bytes(recv_e.at[pl.ds(0, LZ - 1)], rsem.at[4])
            ends_t = recv_e[...].reshape(NT, 128).T
            ends[0] = ends_t[:NS]
            ends[1] = ends_t[NS:]

            def finish(kg, carry):
                for i in range(8):
                    k = kg * 8 + i
                    for ph, m1, m2 in ((0, 3, 2), (1, 5, 4)):
                        c1 = coef[m1, kg, i : i + 1, :]
                        c2_ = coef[m2, kg, i : i + 1, :]
                        high, low = split(snap0[ph * NZ + k] + c1 * ends[0] + c2_ * ends[1])
                        snap[ph * NZ + k, :NS, :] = high
                        snap[ph * NZ + k, NS:, :] = low
                return carry

            lax.fori_loop(0, NZ // 8, finish, 0)
            pltpu.make_async_copy(snap, snap_out, out_sem).start()
        for h in range(2):
            slot = 6 + 2 * phase + h
            await_bytes(recv_h.at[phase, h, pl.ds(0, 7)], rsem.at[slot])
        halves = [add([recv_h[phase, h, i] for i in range(8)]) for h in range(2)]
    gram_out[...] = jnp.concatenate(halves, axis=0)

    await_bytes(recv_c.at[pl.ds(0, LZ - 1)], ssem.at[0])
    await_bytes(recv_bu.at[0, pl.ds(0, LZ - 1)], ssem.at[1])
    await_bytes(recv_bu.at[1, pl.ds(0, LZ - 1)], ssem.at[2])
    await_bytes(recv_x.at[pl.ds(0, LX - 1)], ssem.at[3])
    await_bytes(recv_e.at[pl.ds(0, LZ - 1)], ssem.at[4])
    await_bytes(recv_g.at[pl.ds(0, 2 * LX - 1)], ssem.at[5])
    for slot in range(6, 10):
        await_bytes(recv_h.at[0, 0, pl.ds(0, 7)], ssem.at[slot])
    pltpu.make_async_copy(snap, snap_out, out_sem).wait()


def reciprocal(d):
    r = pl.reciprocal(d, approx=True)
    r = r * (2.0 - d * r)
    return r * (2.0 - d * r)


def eliminate(gram):
    rows_i = lax.broadcasted_iota(jnp.int32, (8, 128), 0)
    lane_i = lax.broadcasted_iota(jnp.int32, (8, 128), 1)
    w = []
    for b in range(8):
        part = gram[(b % 4) * 8 : (b % 4) * 8 + 8, :]
        if b >= 4:
            part = pltpu.roll(part, NS, 1)
        eye = (lane_i == rows_i + (NS + 8 * b)).astype(F32)
        w.append(jnp.where(lane_i < NS, part, eye))
    done = []
    for step in range(16):
        b, s0 = divmod(4 * step, 8)
        full = (8, 128)
        r = [jnp.broadcast_to(w[b][s0 + i : s0 + i + 1, :], full) for i in range(4)]
        d = {
            (i, j): jnp.broadcast_to(r[i][:, 4 * step + j : 4 * step + j + 1], full)
            for i in range(4) for j in range(i, 4)
        }
        low, inv, piv = {}, [], []
        for i in range(4):
            inv.append(reciprocal(d[i, i]))
            piv.append(d[i, i])
            for j in range(i + 1, 4):
                low[j, i] = d[i, j] * inv[i]
            for j in range(i + 1, 4):
                for m in range(j, 4):
                    d[j, m] = d[j, m] - low[j, i] * d[i, m]
                r[j] = r[j] - low[j, i] * r[i]
        for i in range(4):
            done.append(r[i] * lax.rsqrt(piv[i]))
        t = [None] * 4
        for i in reversed(range(4)):
            t[i] = inv[i] * r[i]
            for j in range(i + 1, 4):
                t[i] = t[i] - low[j, i] * t[j]
        first = b if s0 == 0 else b + 1
        for g in range(first, 8):
            cols = [jnp.broadcast_to(w[g][:, 4 * step + i : 4 * step + i + 1], full) for i in range(4)]
            w[g] = w[g] - ((cols[0] * t[0] + cols[1] * t[1]) + (cols[2] * t[2] + cols[3] * t[3]))
    out = []
    for b in range(8):
        rows = done[8 * b]
        for s in range(1, 8):
            rows = jnp.where(rows_i == s, done[8 * b + s], rows)
        out.append(rows)
    return jnp.concatenate(out, axis=0)


CHUNKS = 8


def basis_kernel(root, gram, snap_in, basis, factor, snap, out, in_sem, out_sem):
    per = 2 * NZ // CHUNKS
    loads = [
        pltpu.make_async_copy(snap_in.at[pl.ds(i * per, per)], snap.at[pl.ds(i * per, per)], in_sem.at[i])
        for i in range(CHUNKS)
    ]
    for load in loads:
        load.start()
    rows = eliminate(gram)
    upper = lax.broadcasted_iota(jnp.int32, (NS, NS), 1) >= lax.broadcasted_iota(jnp.int32, (NS, NS), 0)
    factor[...] = jnp.where(upper, rows[:, :NS] * (1.0 / root), 0.0)
    high, low = split(rows[:, NS:] * root)
    lhs = jnp.concatenate([high, high, low], axis=1)
    stores = []
    for i in range(CHUNKS):
        loads[i].wait()
        for k in range(i * per, i * per + per):
            both = snap[k]
            rhs = jnp.concatenate([both, both[:NS]], axis=0)
            res = jnp.dot(lhs, rhs, preferred_element_type=F32)
            for h in range(2):
                out[h, pl.ds(k, NS, stride=2 * NZ), :] = res[:, h * 128 : h * 128 + 128]
        ph, z0 = divmod(i * per, NZ)
        for h in range(2):
            copy = pltpu.make_async_copy(
                out.at[h].reshape(NS, 2 * NZ, 128).at[:, pl.ds(i * per, per), :],
                basis.at[:, ph, pl.ds(z0, per), pl.ds(h * 128, 128)], out_sem.at[h, i])
            copy.start()
            stores.append(copy)
    for copy in stores:
        copy.wait()


def per_device(total_rows, solid_start, inlet, ntu, solid_rate):
    vm, dma = pltpu.VMEM, pltpu.SemaphoreType.DMA
    anywhere = pl.BlockSpec(memory_space=pl.ANY)
    invmem = pl.BlockSpec(memory_space=pltpu.VMEM)
    gram, snap = pl.pallas_call(
        sweep_kernel,
        out_shape=(
            jax.ShapeDtypeStruct((32, 128), F32),
            jax.ShapeDtypeStruct((2 * NZ, 2 * NS, NT), BF16),
        ),
        in_specs=[anywhere] * 4,
        out_specs=(invmem, anywhere),
        scratch_shapes=[
            vm((NS, NZ, NT), BF16),
            vm((NZ, NT), F32),
            vm((NZ, NT), F32),
            vm((NS, NT), F32),
            vm((2, NS * NZ, 128), F32),
            vm((7, NZ // 8, 8, NT), F32),
            vm((2 * NZ, NS, NT), F32),
            vm((4, NS, NT), F32),
            vm((2 * NZ, 2 * NS, NT), BF16),
            vm((2, 8, 128), F32),
            vm((2, LZ, SLICE, 128), F32),
            vm((2, SLICE, 128), F32),
            vm((LZ, SLICE, 128), F32),
            vm((32, 128), F32),
            vm((2, 2, 16, 128), F32),
            vm((LZ, 8, 128), F32),
            vm((2, LZ, SLICE, 128), F32),
            vm((LX, 2, SLICE, 128), F32),
            vm((LZ, SLICE, 128), F32),
            vm((2 * LX, 32, 128), F32),
            vm((2, 2, 8, 16, 128), F32),
            vm((128, 64), F32),
            vm((LZ, SLICE, 128), F32),
            vm((8, 128), F32),
            dma((4,)),
            dma,
            dma((10,)),
            dma((10,)),
        ],
        name="sweep",
        compiler_params=pltpu.CompilerParams(
            collective_id=0, has_side_effects=True, vmem_limit_bytes=40 << 20),
    )(solid_start, inlet, ntu, solid_rate)
    root = float(total_rows) ** 0.5
    basis, factor = pl.pallas_call(
        functools.partial(basis_kernel, root),
        out_shape=(
            jax.ShapeDtypeStruct((NS, 2, NZ, NT), F32),
            jax.ShapeDtypeStruct((NS, NS), F32),
        ),
        in_specs=[invmem, anywhere],
        out_specs=(anywhere, invmem),
        scratch_shapes=[
            vm((2 * NZ, 2 * NS, NT), BF16),
            vm((2, NS * 2 * NZ, 128), F32),
            dma((CHUNKS,)),
            dma((2, CHUNKS)),
        ],
        name="basis",
        compiler_params=pltpu.CompilerParams(vmem_limit_bytes=40 << 20),
    )(gram, snap)
    return basis, factor


def solution(mesh):
    placed = (P(None, "ax", "tr"), P(None, "tr"), P("ax", "tr"), P("ax", "tr"))
    total_rows = 2 * NZ * mesh.shape["ax"] * NT * mesh.shape["tr"]
    return jax.shard_map(
        functools.partial(per_device, total_rows),
        mesh=mesh,
        in_specs=placed,
        out_specs=(P(None, None, "ax", "tr"), P()),
        check_vma=False,
    )
```

```python
import functools

import jax
import jax.numpy as jnp
from jax import lax
from jax.experimental import pallas as pl
from jax.experimental.pallas import tpu as pltpu
from jax.sharding import PartitionSpec as P

MESH = pl.DeviceIdType.MESH
F32 = jnp.float32
BF16 = jnp.bfloat16
NS = 64
NZ = 32
NT = 256
LZ, LX, LY = 8, 4, 8
SLICE = NT // LZ


def split(value):
    high = value.astype(BF16)
    low = (value - high.astype(F32)).astype(BF16)
    return high, low


def place():
    ax, tr = lax.axis_index("ax"), lax.axis_index("tr")
    return ax // LZ, lax.rem(ax, LZ), tr // 2, lax.rem(tr, 2)


def device(x, z, y, c):
    return {"ax": x * LZ + z, "tr": y * 2 + c}


def ring(count, body):
    def step(j, carry):
        away = (j + 1) // 2
        body(count // 2 + away * (1 - 2 * lax.rem(j + 1, 2)))
        return carry

    lax.fori_loop(0, count - 1, step, 0)


def await_bytes(ref, sem):
    pltpu.make_async_copy(ref, ref, sem).wait()


def sweep_kernel(
    solid, inlet, ntu, rate,
    gram_out, snap,
    xb, ntu_v, rate_v, inlet_v, xs, coef, snap0, ends,
    send_c, send_bu, send_x, send_e, send_g, send_h,
    recv_c, recv_bu, recv_x, recv_e, recv_g, recv_h,
    coef_t, inlet_t, load_sem, ssem, rsem,
):
    x, z, y, c = place()
    xc = x * 2 + c

    loads = [
        pltpu.make_async_copy(src, dst, load_sem.at[i])
        for i, (src, dst) in enumerate(
            [(ntu, ntu_v), (rate, rate_v), (solid, xb), (inlet, inlet_v)]
        )
    ]
    for load in loads:
        load.start()

    def peer_z(i):
        return lax.rem(z + i, LZ)

    def peer_y(i):
        return lax.rem(y + i, LY)

    def peer_xc(i):
        return lax.rem(xc + i, 2 * LX)

    def dev_z(i):
        return device(x, peer_z(i), y, c)

    def dev_y(i):
        return device(x, z, peer_y(i), c)

    def dev_xc(i):
        p = peer_xc(i)
        return device(p // 2, z, y, lax.rem(p, 2))

    barrier = pltpu.get_barrier_semaphore()
    for count, dev in ((LZ, dev_z), (2 * LX, dev_xc), (LY, dev_y)):
        ring(count, lambda i, dev=dev: pl.semaphore_signal(
            barrier, inc=1, device_id=dev(i), device_id_type=MESH))

    loads[0].wait()
    loads[1].wait()
    n_all = ntu_v[...]
    r_all = rate_v[...]
    a_all = 1.0 / (1.0 + n_all)
    s_all = n_all / (1.0 + n_all)
    coef[0] = a_all.reshape(NZ // 8, 8, NT)
    coef[1] = s_all.reshape(NZ // 8, 8, NT)
    coef[6] = r_all.reshape(NZ // 8, 8, NT)
    sr_all = s_all * r_all
    p = jnp.ones((1, NT), F32)
    q = jnp.zeros((1, NT), F32)
    for k in range(NZ):
        a = a_all[k : k + 1]
        p = a * p
        q = a * q + sr_all[k : k + 1] * p
        coef[2, k // 8, k % 8 : k % 8 + 1, :] = p
        coef[3, k // 8, k % 8 : k % 8 + 1, :] = q
    p_all = coef[2].reshape(NZ, NT)
    q_all = coef[3].reshape(NZ, NT)
    bw = r_all * p_all
    aw = (1.0 - r_all) * bw + r_all * q_all
    coef[4] = bw.reshape(NZ // 8, 8, NT)
    coef[5] = aw.reshape(NZ // 8, 8, NT)
    both = lambda u: jnp.sum(u, axis=0, keepdims=True)
    rows = jnp.concatenate(
        [
            p, q,
            0.5 * both(q_all * q_all + aw * aw),
            both(q_all * p_all + aw * bw),
            0.5 * both(p_all * p_all + bw * bw),
            jnp.zeros((3, NT), F32),
        ],
        axis=0,
    )
    send_c[0] = rows[:, :128]
    send_c[1] = rows[:, 128:]

    loads[2].wait()
    chunk = 16

    def widen(i, carry):
        part = xb[pl.ds(i * 8, 8)].astype(F32)
        for h in range(2):
            for g in range(NZ // 8):
                tile = part[:, g * 8 : g * 8 + 8, h * 128 : h * 128 + 128]
                xs[h, g, pl.ds(pl.multiple_of(i * 64, 64), 64), :] = tile.reshape(64, 128)
        return carry

    lax.fori_loop(0, NS // 8, widen, 0)

    def sweep_chunk(ci, carry):
        n0 = ci * chunk

        def plane(kg, i, state):
            new = []
            k = kg * 8 + i
            for h in range(2):
                f1, f2, u1, u2 = state[h]
                lanes = pl.ds(h * 128, 128)
                one = lambda m: jnp.broadcast_to(coef[m, kg, i : i + 1, lanes], (chunk, 128))
                a, s, pp, qq, bb, aa, r = (one(m) for m in range(7))
                v = xs[h, kg, pl.ds(n0 * 8 + i, chunk, stride=8), :]
                f1 = a * f1 + s * v
                v = v + r * (f1 - v)
                f2 = a * f2 + s * v
                w = v + r * (f2 - v)
                snap0[k, pl.ds(n0, chunk), lanes] = f2
                snap0[NZ + k, pl.ds(n0, chunk), lanes] = w
                u1 = u1 + (qq * f2 + aa * w)
                u2 = u2 + (pp * f2 + bb * w)
                new.append((f1, f2, u1, u2))
            return tuple(new)

        def planes(kg, state):
            for i in range(8):
                state = plane(kg, i, state)
            return state

        zero = jnp.zeros((chunk, 128), F32)
        state = lax.fori_loop(0, NZ // 8, planes, ((zero,) * 4,) * 2)
        for h in range(2):
            for m in range(4):
                ends[m, pl.ds(n0, chunk), h * 128 : h * 128 + 128] = state[h][m]
        return carry

    lax.fori_loop(0, NS // chunk, sweep_chunk, 0)
    for m in range(2):
        flat = jnp.concatenate([ends[2 * m], ends[2 * m + 1]], axis=0)
        send_bu[m] = flat.T.reshape(LZ, SLICE, 128)

    pl.semaphore_wait(barrier, (LZ - 1) + (2 * LX - 1) + (LY - 1))

    ring(LZ, lambda i: pltpu.make_async_remote_copy(
        send_c.at[peer_z(i) // 4], recv_c.at[z], ssem.at[0], rsem.at[0],
        device_id=dev_z(i), device_id_type=MESH).start())
    for m in range(2):
        ring(LZ, lambda i: pltpu.make_async_remote_copy(
            send_bu.at[m, peer_z(i)], recv_bu.at[m, z], ssem.at[1 + m], rsem.at[1 + m],
            device_id=dev_z(i), device_id_type=MESH).start())
    recv_c[z] = send_c[z // 4]
    recv_bu[0, z] = send_bu[0, z]
    recv_bu[1, z] = send_bu[1, z]

    loads[3].wait()
    inl = inlet_v[...]
    inlet_t[...] = jnp.concatenate([inl, inl], axis=0).T.reshape(LZ, SLICE, 128)

    def inner(k, acc):
        high, low = split(snap0[k])
        rowsb = jnp.concatenate([high, low], axis=0)
        return acc + lax.dot_general(rowsb, rowsb, (((1,), (1,)), ((), ())), preferred_element_type=F32)

    acc = lax.fori_loop(0, 2 * NZ, inner, jnp.zeros((2 * NS, 2 * NS), F32), unroll=4)
    gram0 = (acc[:NS, :NS] + acc[NS:, NS:]) + (acc[:NS, NS:] + acc[NS:, :NS])

    await_bytes(recv_c.at[pl.ds(0, LZ - 1)], rsem.at[0])
    coef_t[...] = recv_c[...].reshape(LZ * 8, 128).T
    ct = coef_t[pl.ds(pl.multiple_of(lax.rem(z, 4) * SLICE, SLICE), SLICE), :]
    lane = lax.broadcasted_iota(jnp.int32, (SLICE, 128), 1)
    second = lane >= NS
    wide = lambda k, m: jnp.broadcast_to(ct[:, k * 8 + m : k * 8 + m + 1], (SLICE, 128))
    turn = lambda u: pltpu.roll(u, NS, 1)
    aks = [wide(k, 0) for k in range(LZ)]
    cks = [wide(k, 1) for k in range(LZ)]
    c2s = [jnp.where(second, ck, 0.0) for ck in cks]
    await_bytes(recv_bu.at[0, pl.ds(0, LZ - 1)], rsem.at[1])
    bks = [recv_bu[0, k] for k in range(LZ)]
    bds = [jnp.where(second, turn(b), b) for b in bks]
    full, dup, at, ctot = bks[0], bds[0], aks[0], cks[0]
    for k in range(1, LZ):
        full, dup = aks[k] * full + c2s[k] * dup + bks[k], aks[k] * dup + bds[k]
        at, ctot = aks[k] * at, aks[k] * ctot + cks[k] * at
    send_x[0] = full
    send_x[1] = jnp.where(second, ctot, at)

    def send_line(i):
        px = lax.rem(x + i, LX)
        pltpu.make_async_remote_copy(
            send_x, recv_x.at[x], ssem.at[3], rsem.at[3],
            device_id=device(px, z, y, c), device_id_type=MESH).start()

    ring(LX, send_line)
    recv_x[x] = send_x[...]
    await_bytes(recv_x.at[pl.ds(0, LX - 1)], rsem.at[3])
    e = inlet_t[z]
    d = e
    for k in range(LX - 1):
        f, cf = recv_x[k, 0], recv_x[k, 1]
        rolled = turn(cf)
        a = jnp.where(second, rolled, cf)
        c2 = jnp.where(second, cf, 0.0)
        fd = jnp.where(second, turn(f), f)
        e_new = a * e + c2 * d + f
        d_new = a * d + fd
        upstream = jnp.full((SLICE, 128), k, jnp.int32) < x
        e = jnp.where(upstream, e_new, e)
        d = jnp.where(upstream, d_new, d)
    for k in range(LZ):
        send_e[k] = e
        if k < LZ - 1:
            e, d = aks[k] * e + c2s[k] * d + bks[k], aks[k] * d + bds[k]
    ring(LZ, lambda i: pltpu.make_async_remote_copy(
        send_e.at[peer_z(i)], recv_e.at[z], ssem.at[4], rsem.at[4],
        device_id=dev_z(i), device_id_type=MESH).start())
    recv_e[z] = send_e[z]

    await_bytes(recv_bu.at[1, pl.ds(0, LZ - 1)], rsem.at[2])
    vs = []
    for k in range(LZ):
        ek = send_e[k]
        hk = jnp.where(second, wide(k, 4), wide(k, 2))
        abk = jnp.where(second, 0.0, wide(k, 3))
        vs.append(recv_bu[1, k] + hk * ek + abk * turn(ek))
    vh, vl = split(jnp.concatenate(vs, axis=0))
    eh, el = split(send_e[...].reshape(LZ * SLICE, 128))
    prod = lax.dot_general(
        jnp.concatenate([vh, vl], axis=1), jnp.concatenate([eh, el], axis=1),
        (((0,), (0,)), ((), ())), preferred_element_type=F32)
    prod = (prod[:128, :128] + prod[128:, 128:]) + (prod[:128, 128:] + prod[128:, :128])
    cross = prod[:NS, :NS] + prod[NS:, NS:]
    gram = gram0 + (cross + cross.T)
    send_g[...] = jnp.concatenate([gram[: NS // 2], gram[NS // 2 :]], axis=1)

    ring(2 * LX, lambda i: pltpu.make_async_remote_copy(
        send_g, recv_g.at[xc], ssem.at[5], rsem.at[5],
        device_id=dev_xc(i), device_id_type=MESH).start())
    recv_g[xc] = send_g[...]
    await_bytes(recv_g.at[pl.ds(0, 2 * LX - 1)], rsem.at[5])

    def add(parts):
        while len(parts) > 1:
            parts = [parts[i] + parts[i + 1] for i in range(0, len(parts), 2)]
        return parts[0]

    sums = add([recv_g[i] for i in range(2 * LX)])
    halves = [sums[:16], sums[16:]]
    for phase in range(2):
        for h in range(2):
            send_h[phase, h] = halves[h]
        for h in range(2):
            over_z = (h + phase) % 2 == 0
            dev, mine = (dev_z, z) if over_z else (dev_y, y)
            slot = 6 + 2 * phase + h
            ring(8, lambda i, dev=dev, mine=mine, slot=slot, h=h: pltpu.make_async_remote_copy(
                send_h.at[phase, h], recv_h.at[phase, h, mine], ssem.at[slot], rsem.at[slot],
                device_id=dev(i), device_id_type=MESH).start())
            recv_h[phase, h, mine] = halves[h]
        if phase == 0:
            await_bytes(recv_e.at[pl.ds(0, LZ - 1)], rsem.at[4])
            ends_t = recv_e[...].reshape(NT, 128).T
            ends[0] = ends_t[:NS]
            ends[1] = ends_t[NS:]

            def finish(kg, carry):
                for i in range(8):
                    k = kg * 8 + i
                    for ph, m1, m2 in ((0, 3, 2), (1, 5, 4)):
                        c1 = coef[m1, kg, i : i + 1, :]
                        c2_ = coef[m2, kg, i : i + 1, :]
                        high, low = split(snap0[ph * NZ + k] + c1 * ends[0] + c2_ * ends[1])
                        snap[ph * NZ + k, :NS, :] = high
                        snap[ph * NZ + k, NS:, :] = low
                return carry

            lax.fori_loop(0, NZ // 8, finish, 0)
        for h in range(2):
            slot = 6 + 2 * phase + h
            await_bytes(recv_h.at[phase, h, pl.ds(0, 7)], rsem.at[slot])
        halves = [add([recv_h[phase, h, i] for i in range(8)]) for h in range(2)]
    gram_out[...] = jnp.concatenate(halves, axis=0)

    await_bytes(recv_c.at[pl.ds(0, LZ - 1)], ssem.at[0])
    await_bytes(recv_bu.at[0, pl.ds(0, LZ - 1)], ssem.at[1])
    await_bytes(recv_bu.at[1, pl.ds(0, LZ - 1)], ssem.at[2])
    await_bytes(recv_x.at[pl.ds(0, LX - 1)], ssem.at[3])
    await_bytes(recv_e.at[pl.ds(0, LZ - 1)], ssem.at[4])
    await_bytes(recv_g.at[pl.ds(0, 2 * LX - 1)], ssem.at[5])
    for slot in range(6, 10):
        await_bytes(recv_h.at[0, 0, pl.ds(0, 7)], ssem.at[slot])


def reciprocal(d):
    r = pl.reciprocal(d, approx=True)
    return r * (2.0 - d * r)


def rsqrt(d):
    r = lax.rsqrt(d)
    return r * (1.5 - (0.5 * d * r) * r)


def eliminate(gram):
    full = (8, 128)
    rows_i = lax.broadcasted_iota(jnp.int32, full, 0)
    lane_i = lax.broadcasted_iota(jnp.int32, full, 1)
    left = lane_i < NS
    w, on_rows, on_lanes = [], [], jnp.zeros(full, F32)
    for b in range(8):
        part = gram[(b % 4) * 8 : (b % 4) * 8 + 8, :]
        if b >= 4:
            part = pltpu.roll(part, NS, 1)
        diag = jnp.where(lane_i == rows_i + 8 * b, part, 0.0)
        on_rows.append(jnp.broadcast_to(jnp.sum(diag, axis=1, keepdims=True), full))
        on_lanes = on_lanes + diag
        w.append(part)
    on_lanes = jnp.broadcast_to(jnp.sum(on_lanes, axis=0, keepdims=True), full)
    on_lanes = jnp.where(left, on_lanes, pltpu.roll(on_lanes, NS, 1))
    unit = rsqrt(on_lanes)
    undo = jnp.where(left, on_lanes * unit, unit)
    for b in range(8):
        eye = (lane_i == rows_i + (NS + 8 * b)).astype(F32)
        w[b] = jnp.where(left, w[b] * (rsqrt(on_rows[b]) * unit), eye)
    out = []
    for b in range(8):
        r = [jnp.broadcast_to(w[b][i : i + 1, :], full) for i in range(8)]
        column = lambda u, i: jnp.broadcast_to(u[:, 8 * b + i : 8 * b + i + 1], full)
        d = {(i, j): column(r[i], j) for i in range(8) for j in range(i, 8)}
        cols = {g: [column(w[g], i) for i in range(8)] for g in range(b + 1, 8)}
        done = []
        for i in range(0, 8, 2):
            k = i + 1
            d00, d01, d11 = d[i, i], d[i, k], d[k, k]
            det = d00 * d11 - d01 * d01
            inv = reciprocal(det)
            a00, a01, a11 = d11 * inv, d01 * inv, d00 * inv
            y = {}
            for j in range(i + 2, 8):
                y[j] = (a00 * d[i, j] - a01 * d[k, j], a11 * d[k, j] - a01 * d[i, j])
            x0 = a00 * r[i] - a01 * r[k]
            x1 = a11 * r[k] - a01 * r[i]
            for j in range(i + 2, 8):
                for m in range(j, 8):
                    d[j, m] = d[j, m] - (d[i, j] * y[m][0] + d[k, j] * y[m][1])
                r[j] = r[j] - (d[i, j] * x0 + d[k, j] * x1)
            for g in range(b + 1, 8):
                c = cols[g]
                w[g] = w[g] - (c[i] * x0 + c[k] * x1)
                for j in range(i + 2, 8):
                    c[j] = c[j] - (c[i] * y[j][0] + c[k] * y[j][1])
            done.append(r[i] * rsqrt(d00))
            done.append((d00 * r[k] - d01 * r[i]) * rsqrt(d00 * det))
        rows = done[0]
        for s in range(1, 8):
            rows = jnp.where(rows_i == s, done[s], rows)
        out.append(rows * undo)
    return jnp.concatenate(out, axis=0)


CHUNKS = 8


def basis_kernel(root, gram, snap, basis, factor, out, out_sem):
    per = 2 * NZ // CHUNKS
    rows = eliminate(gram)
    upper = lax.broadcasted_iota(jnp.int32, (NS, NS), 1) >= lax.broadcasted_iota(jnp.int32, (NS, NS), 0)
    factor[...] = jnp.where(upper, rows[:, :NS] * (1.0 / root), 0.0)
    high, low = split(rows[:, NS:] * root)
    lhs = jnp.concatenate([high, high, low], axis=1)
    stores = []
    for i in range(CHUNKS):
        for k in range(i * per, i * per + per):
            both = snap[k]
            rhs = jnp.concatenate([both, both[:NS]], axis=0)
            res = jnp.dot(lhs, rhs, preferred_element_type=F32)
            for h in range(2):
                out[h, i, pl.ds(k - i * per, NS, stride=8), :] = res[:, h * 128 : h * 128 + 128]
        ph, z0 = divmod(i * per, NZ)
        for h in range(2):
            copy = pltpu.make_async_copy(
                out.at[h, i].reshape(NS, 8, 128),
                basis.at[:, ph, pl.ds(z0, per), pl.ds(h * 128, 128)], out_sem.at[h, i])
            copy.start()
            stores.append(copy)
    for copy in stores:
        copy.wait()


def basis_call(total_rows, gram, snap):
    vm, dma = pltpu.VMEM, pltpu.SemaphoreType.DMA
    anywhere = pl.BlockSpec(memory_space=pl.ANY)
    invmem = pl.BlockSpec(memory_space=pltpu.VMEM)
    root = float(total_rows) ** 0.5
    return pl.pallas_call(
        functools.partial(basis_kernel, root),
        out_shape=(
            jax.ShapeDtypeStruct((NS, 2, NZ, NT), F32),
            jax.ShapeDtypeStruct((NS, NS), F32),
        ),
        in_specs=[invmem, invmem],
        out_specs=(anywhere, invmem),
        scratch_shapes=[
            vm((2, CHUNKS, NS * 8, 128), F32),
            dma((2, CHUNKS)),
        ],
        name="basis",
        compiler_params=pltpu.CompilerParams(vmem_limit_bytes=40 << 20),
    )(gram, snap)


def per_device(total_rows, solid_start, inlet, ntu, solid_rate):
    vm, dma = pltpu.VMEM, pltpu.SemaphoreType.DMA
    anywhere = pl.BlockSpec(memory_space=pl.ANY)
    invmem = pl.BlockSpec(memory_space=pltpu.VMEM)
    gram, snap = pl.pallas_call(
        sweep_kernel,
        out_shape=(
            jax.ShapeDtypeStruct((32, 128), F32),
            jax.ShapeDtypeStruct((2 * NZ, 2 * NS, NT), BF16),
        ),
        in_specs=[pl.BlockSpec(memory_space=pltpu.HBM)] * 4,
        out_specs=(invmem, invmem),
        scratch_shapes=[
            vm((NS, NZ, NT), BF16),
            vm((NZ, NT), F32),
            vm((NZ, NT), F32),
            vm((NS, NT), F32),
            vm((2, NZ // 8, NS * 8, 128), F32),
            vm((7, NZ // 8, 8, NT), F32),
            vm((2 * NZ, NS, NT), F32),
            vm((4, NS, NT), F32),
            vm((2, 8, 128), F32),
            vm((2, LZ, SLICE, 128), F32),
            vm((2, SLICE, 128), F32),
            vm((LZ, SLICE, 128), F32),
            vm((32, 128), F32),
            vm((2, 2, 16, 128), F32),
            vm((LZ, 8, 128), F32),
            vm((2, LZ, SLICE, 128), F32),
            vm((LX, 2, SLICE, 128), F32),
            vm((LZ, SLICE, 128), F32),
            vm((2 * LX, 32, 128), F32),
            vm((2, 2, 8, 16, 128), F32),
            vm((128, 64), F32),
            vm((LZ, SLICE, 128), F32),
            dma((4,)),
            dma((10,)),
            dma((10,)),
        ],
        name="sweep",
        compiler_params=pltpu.CompilerParams(
            collective_id=0, has_side_effects=True, vmem_limit_bytes=40 << 20),
    )(*(pltpu.with_memory_space_constraint(v, pltpu.HBM) for v in (solid_start, inlet, ntu, solid_rate)))
    basis, factor = basis_call(total_rows, gram, snap)
    return basis, factor


def solution(mesh):
    placed = (P(None, "ax", "tr"), P(None, "tr"), P("ax", "tr"), P("ax", "tr"))
    total_rows = 2 * NZ * mesh.shape["ax"] * NT * mesh.shape["tr"]
    return jax.shard_map(
        functools.partial(per_device, total_rows),
        mesh=mesh,
        in_specs=placed,
        out_specs=(P(None, None, "ax", "tr"), P()),
        check_vma=False,
    )
```

```python
import functools

import jax
import jax.numpy as jnp
from jax import lax
from jax.experimental import pallas as pl
from jax.experimental.pallas import tpu as pltpu
from jax.sharding import PartitionSpec as P

MESH = pl.DeviceIdType.MESH
F32 = jnp.float32
BF16 = jnp.bfloat16
NS = 64
NZ = 32
NT = 256
LZ, LX, LY = 8, 4, 8
SLICE = NT // LZ


def split(value):
    high = value.astype(BF16)
    low = (value - high.astype(F32)).astype(BF16)
    return high, low


def place():
    ax, tr = lax.axis_index("ax"), lax.axis_index("tr")
    return ax // LZ, lax.rem(ax, LZ), tr // 2, lax.rem(tr, 2)


def device(x, z, y, c):
    return {"ax": x * LZ + z, "tr": y * 2 + c}


def ring(count, body):
    def step(j, carry):
        away = (j + 1) // 2
        body(count // 2 + away * (1 - 2 * lax.rem(j + 1, 2)))
        return carry

    lax.fori_loop(0, count - 1, step, 0)


def await_bytes(ref, sem):
    pltpu.make_async_copy(ref, ref, sem).wait()


def sweep_kernel(
    solid, inlet, ntu, rate,
    gram_out, snap,
    xb, ntu_v, rate_v, inlet_v, xs, coef, snap0, ends,
    send_c, send_bu, send_x, send_e, send_g, send_h,
    recv_c, recv_bu, recv_x, recv_e, recv_g, recv_h,
    coef_t, inlet_t, load_sem, ssem, rsem,
):
    x, z, y, c = place()
    xc = x * 2 + c

    loads = [
        pltpu.make_async_copy(src, dst, load_sem.at[i])
        for i, (src, dst) in enumerate(
            [(ntu, ntu_v), (rate, rate_v), (solid, xb), (inlet, inlet_v)]
        )
    ]
    def peer_z(i):
        return lax.rem(z + i, LZ)

    def peer_y(i):
        return lax.rem(y + i, LY)

    def peer_xc(i):
        return lax.rem(xc + i, 2 * LX)

    def dev_z(i):
        return device(x, peer_z(i), y, c)

    def dev_y(i):
        return device(x, z, peer_y(i), c)

    def dev_xc(i):
        p = peer_xc(i)
        return device(p // 2, z, y, lax.rem(p, 2))

    barrier = pltpu.get_barrier_semaphore()
    for at, (count, dev) in enumerate(((LZ, dev_z), (2 * LX, dev_xc), (LY, dev_y))):
        if at == 1:
            for load in loads:
                load.start()
        ring(count, lambda i, dev=dev: pl.semaphore_signal(
            barrier, inc=1, device_id=dev(i), device_id_type=MESH))

    loads[0].wait()
    loads[1].wait()
    n_all = ntu_v[...]
    r_all = rate_v[...]
    a_all = 1.0 / (1.0 + n_all)
    s_all = n_all * a_all
    sr_all = s_all * r_all
    row = lax.broadcasted_iota(jnp.int32, (8, NT), 0)
    shift = lambda u, k, fill: jnp.where(row >= k, pltpu.roll(u, k, 0), fill)
    groups = range(NZ // 8)
    scales = [[a_all[g * 8 : g * 8 + 8]] for g in groups]
    for k in (1, 2, 4):
        for scale in scales:
            scale.append(scale[-1] * shift(scale[-1], k, 1.0))
    p_all, q_all = [], []
    for g in groups:
        p_all.append(scales[g][3] * p_all[-1][7:8] if g else scales[g][3])
        q = sr_all[g * 8 : g * 8 + 8] * p_all[g]
        for step, k in enumerate((1, 2, 4)):
            q = q + scales[g][step] * shift(q, k, 0.0)
        q_all.append(q)
    for g in groups[1:]:
        q_all[g] = q_all[g] + scales[g][3] * q_all[g - 1][7:8]
    p, q = p_all[-1][7:8], q_all[-1][7:8]
    p_all, q_all = jnp.concatenate(p_all, axis=0), jnp.concatenate(q_all, axis=0)
    for m, u in enumerate((a_all, s_all, p_all, q_all)):
        coef[m] = u.reshape(NZ // 8, 8, NT)
    coef[6] = r_all.reshape(NZ // 8, 8, NT)
    bw = r_all * p_all
    aw = (1.0 - r_all) * bw + r_all * q_all
    coef[4] = bw.reshape(NZ // 8, 8, NT)
    coef[5] = aw.reshape(NZ // 8, 8, NT)
    both = lambda u: jnp.sum(u, axis=0, keepdims=True)
    rows = jnp.concatenate(
        [
            p, q,
            0.5 * both(q_all * q_all + aw * aw),
            both(q_all * p_all + aw * bw),
            0.5 * both(p_all * p_all + bw * bw),
            jnp.zeros((3, NT), F32),
        ],
        axis=0,
    )
    send_c[0] = rows[:, :128]
    send_c[1] = rows[:, 128:]

    loads[2].wait()
    chunk = 16

    def widen(i, carry):
        part = xb[pl.ds(i * 8, 8)].astype(F32)
        for h in range(2):
            for g in range(NZ // 8):
                tile = part[:, g * 8 : g * 8 + 8, h * 128 : h * 128 + 128]
                xs[h, g, pl.ds(pl.multiple_of(i * 64, 64), 64), :] = tile.reshape(64, 128)
        return carry

    lax.fori_loop(0, NS // 8, widen, 0)

    def sweep_chunk(ci, carry):
        n0 = ci * chunk

        def plane(kg, i, state):
            new = []
            k = kg * 8 + i
            for h in range(2):
                f1, f2, u1, u2 = state[h]
                lanes = pl.ds(h * 128, 128)
                one = lambda m: jnp.broadcast_to(coef[m, kg, i : i + 1, lanes], (chunk, 128))
                a, s, pp, qq, bb, aa, r = (one(m) for m in range(7))
                v = xs[h, kg, pl.ds(n0 * 8 + i, chunk, stride=8), :]
                f1 = a * f1 + s * v
                v = v + r * (f1 - v)
                f2 = a * f2 + s * v
                w = v + r * (f2 - v)
                snap0[k, pl.ds(n0, chunk), lanes] = f2
                snap0[NZ + k, pl.ds(n0, chunk), lanes] = w
                u1 = u1 + (qq * f2 + aa * w)
                u2 = u2 + (pp * f2 + bb * w)
                new.append((f1, f2, u1, u2))
            return tuple(new)

        def planes(kg, state):
            for i in range(8):
                state = plane(kg, i, state)
            return state

        zero = jnp.zeros((chunk, 128), F32)
        state = lax.fori_loop(0, NZ // 8, planes, ((zero,) * 4,) * 2)
        for h in range(2):
            for m in range(4):
                ends[m, pl.ds(n0, chunk), h * 128 : h * 128 + 128] = state[h][m]
        return carry

    lax.fori_loop(0, NS // chunk, sweep_chunk, 0)
    for m in range(2):
        flat = jnp.concatenate([ends[2 * m], ends[2 * m + 1]], axis=0)
        send_bu[m] = flat.T.reshape(LZ, SLICE, 128)

    pl.semaphore_wait(barrier, (LZ - 1) + (2 * LX - 1) + (LY - 1))

    ring(LZ, lambda i: pltpu.make_async_remote_copy(
        send_c.at[peer_z(i) // 4], recv_c.at[z], ssem.at[0], rsem.at[0],
        device_id=dev_z(i), device_id_type=MESH).start())
    for m in range(2):
        ring(LZ, lambda i: pltpu.make_async_remote_copy(
            send_bu.at[m, peer_z(i)], recv_bu.at[m, z], ssem.at[1 + m], rsem.at[1 + m],
            device_id=dev_z(i), device_id_type=MESH).start())
    recv_c[z] = send_c[z // 4]
    recv_bu[0, z] = send_bu[0, z]
    recv_bu[1, z] = send_bu[1, z]

    loads[3].wait()
    inl = inlet_v[...]
    inlet_t[...] = jnp.concatenate([inl, inl], axis=0).T.reshape(LZ, SLICE, 128)

    def inner(k, acc):
        high, low = split(snap0[k])
        rowsb = jnp.concatenate([high, low], axis=0)
        return acc + lax.dot_general(rowsb, rowsb, (((1,), (1,)), ((), ())), preferred_element_type=F32)

    acc = lax.fori_loop(0, 2 * NZ, inner, jnp.zeros((2 * NS, 2 * NS), F32), unroll=4)
    gram0 = (acc[:NS, :NS] + acc[NS:, NS:]) + (acc[:NS, NS:] + acc[NS:, :NS])

    await_bytes(recv_c.at[pl.ds(0, LZ - 1)], rsem.at[0])
    coef_t[...] = recv_c[...].reshape(LZ * 8, 128).T
    ct = coef_t[pl.ds(pl.multiple_of(lax.rem(z, 4) * SLICE, SLICE), SLICE), :]
    lane = lax.broadcasted_iota(jnp.int32, (SLICE, 128), 1)
    second = lane >= NS
    wide = lambda k, m: jnp.broadcast_to(ct[:, k * 8 + m : k * 8 + m + 1], (SLICE, 128))
    turn = lambda u: pltpu.roll(u, NS, 1)
    first = lambda u: jnp.where(second, 0.0, u)
    aks = [wide(k, 0) for k in range(LZ)]
    cks = [wide(k, 1) for k in range(LZ)]
    c2s = [jnp.where(second, ck, 0.0) for ck in cks]
    at, ctot = aks[0], cks[0]
    reach = [None]
    for k in range(1, LZ):
        reach.append((at, ctot))
        at, ctot = aks[k] * at, aks[k] * ctot + cks[k] * at
    send_x[1] = jnp.where(second, ctot, at)

    def send_line(part):
        def send(i):
            px = lax.rem(x + i, LX)
            pltpu.make_async_remote_copy(
                send_x.at[part], recv_x.at[part, x], ssem.at[3 + 8 * part], rsem.at[3 + 8 * part],
                device_id=device(px, z, y, c), device_id_type=MESH).start()

        ring(LX, send)
        recv_x[part, x] = send_x[part]

    send_line(1)
    await_bytes(recv_bu.at[0, pl.ds(0, LZ - 1)], rsem.at[1])
    bks = [recv_bu[0, k] for k in range(LZ)]
    bds = [jnp.where(second, turn(b), b) for b in bks]
    full, dup = bks[0], bds[0]
    before = [None]
    for k in range(1, LZ):
        before.append((full,) + reach[k])
        full, dup = aks[k] * full + c2s[k] * dup + bks[k], aks[k] * dup + bds[k]
    send_x[0] = full
    send_line(0)

    aas, abs_, bbs = ([wide(k, m) for k in range(LZ)] for m in (2, 3, 4))
    aa, ab, bb = aas[0], abs_[0], bbs[0]
    for k in range(1, LZ):
        _, ah, ch = before[k]
        a2 = ah * ah
        ac = ah * ch
        aa = aa + (aas[k] * a2 + abs_[k] * ac + bbs[k] * (ch * ch))
        ab = ab + (abs_[k] * a2 + 2.0 * bbs[k] * ac)
        bb = bb + bbs[k] * a2
    await_bytes(recv_bu.at[1, pl.ds(0, LZ - 1)], rsem.at[2])
    answer = recv_bu[1, 0]
    vs = []
    for k in range(1, LZ):
        e0, ah, ch = before[k]
        te = turn(e0)
        own = jnp.where(second, bbs[k], aas[k]) * e0
        u = recv_bu[1, k]
        vs.append(u + own + first(abs_[k]) * te)
        w = u + 2.0 * own + abs_[k] * te
        answer = answer + (ah * w + first(ch) * turn(w))

    def cross(v, e):
        vh, vl = split(v)
        eh, el = split(e)
        prod = lax.dot_general(
            jnp.concatenate([vh, vl], axis=1), jnp.concatenate([eh, el], axis=1),
            (((0,), (0,)), ((), ())), preferred_element_type=F32)
        prod = (prod[:128, :128] + prod[128:, 128:]) + (prod[:128, 128:] + prod[128:, :128])
        part = prod[:NS, :NS] + prod[NS:, NS:]
        return part + part.T

    gram1 = gram0 + cross(
        jnp.concatenate(vs, axis=0), jnp.concatenate([before[k][0] for k in range(1, LZ)], axis=0))
    for part in range(2):
        await_bytes(recv_x.at[part, pl.ds(0, LX - 1)], rsem.at[3 + 8 * part])
    e = inlet_t[z]
    d = e
    for k in range(LX - 1):
        f, cf = recv_x[0, k], recv_x[1, k]
        rolled = turn(cf)
        a = jnp.where(second, rolled, cf)
        c2 = jnp.where(second, cf, 0.0)
        fd = jnp.where(second, turn(f), f)
        e_new = a * e + c2 * d + f
        d_new = a * d + fd
        upstream = jnp.full((SLICE, 128), k, jnp.int32) < x
        e = jnp.where(upstream, e_new, e)
        d = jnp.where(upstream, d_new, d)
    gram = gram1 + cross(answer + jnp.where(second, bb, aa) * e + first(ab) * turn(e), e)
    send_g[...] = jnp.concatenate([gram[: NS // 2], gram[NS // 2 :]], axis=1)

    ring(2 * LX, lambda i: pltpu.make_async_remote_copy(
        send_g, recv_g.at[xc], ssem.at[5], rsem.at[5],
        device_id=dev_xc(i), device_id_type=MESH).start())

    for k in range(LZ):
        send_e[k] = e
        if k < LZ - 1:
            e, d = aks[k] * e + c2s[k] * d + bks[k], aks[k] * d + bds[k]
    ring(LZ, lambda i: pltpu.make_async_remote_copy(
        send_e.at[peer_z(i)], recv_e.at[z], ssem.at[4], rsem.at[4],
        device_id=dev_z(i), device_id_type=MESH).start())
    recv_e[z] = send_e[z]
    recv_g[xc] = send_g[...]
    await_bytes(recv_g.at[pl.ds(0, 2 * LX - 1)], rsem.at[5])

    def add(parts):
        while len(parts) > 1:
            parts = [parts[i] + parts[i + 1] for i in range(0, len(parts), 2)]
        return parts[0]

    sums = add([recv_g[i] for i in range(2 * LX)])
    halves = [sums[:16], sums[16:]]
    for phase in range(2):
        for h in range(2):
            send_h[phase, h] = halves[h]
        def send_halves(i):
            for h in range(2):
                over_z = (h + phase) % 2 == 0
                dev, mine, slot = dev_z(i) if over_z else dev_y(i), z if over_z else y, 6 + 2 * phase + h
                pltpu.make_async_remote_copy(
                    send_h.at[phase, h], recv_h.at[phase, h, mine], ssem.at[slot], rsem.at[slot],
                    device_id=dev, device_id_type=MESH).start()

        ring(8, send_halves)
        for h in range(2):
            recv_h[phase, h, z if (h + phase) % 2 == 0 else y] = halves[h]
        if phase == 1:
            await_bytes(recv_e.at[pl.ds(0, LZ - 1)], rsem.at[4])
            ends_t = recv_e[...].reshape(NT, 128).T
            ends[0] = ends_t[:NS]
            ends[1] = ends_t[NS:]

            def finish(kg, carry):
                for i in range(8):
                    k = kg * 8 + i
                    for ph, m1, m2 in ((0, 3, 2), (1, 5, 4)):
                        c1 = coef[m1, kg, i : i + 1, :]
                        c2_ = coef[m2, kg, i : i + 1, :]
                        high, low = split(snap0[ph * NZ + k] + c1 * ends[0] + c2_ * ends[1])
                        snap[ph * NZ + k, :NS, :] = high
                        snap[ph * NZ + k, NS:, :] = low
                return carry

            lax.fori_loop(0, NZ // 8, finish, 0)
        for h in range(2):
            slot = 6 + 2 * phase + h
            await_bytes(recv_h.at[phase, h, pl.ds(0, 7)], rsem.at[slot])
        halves = [add([recv_h[phase, h, i] for i in range(8)]) for h in range(2)]
    gram_out[...] = jnp.concatenate(halves, axis=0)

    await_bytes(recv_c.at[pl.ds(0, LZ - 1)], ssem.at[0])
    await_bytes(recv_bu.at[0, pl.ds(0, LZ - 1)], ssem.at[1])
    await_bytes(recv_bu.at[1, pl.ds(0, LZ - 1)], ssem.at[2])
    for part in range(2):
        await_bytes(recv_x.at[part, pl.ds(0, LX - 1)], ssem.at[3 + 8 * part])
    await_bytes(recv_e.at[pl.ds(0, LZ - 1)], ssem.at[4])
    await_bytes(recv_g.at[pl.ds(0, 2 * LX - 1)], ssem.at[5])
    for slot in range(6, 10):
        await_bytes(recv_h.at[0, 0, pl.ds(0, 7)], ssem.at[slot])


def reciprocal(d):
    r = pl.reciprocal(d, approx=True)
    return r * (2.0 - d * r)


def rsqrt(d):
    r = lax.rsqrt(d)
    return r * (1.5 - (0.5 * d * r) * r)


def eliminate(gram):
    full = (8, 128)
    rows_i = lax.broadcasted_iota(jnp.int32, full, 0)
    lane_i = lax.broadcasted_iota(jnp.int32, full, 1)
    left = lane_i < NS
    w, on_rows, on_lanes = [], [], jnp.zeros(full, F32)
    for b in range(8):
        part = gram[(b % 4) * 8 : (b % 4) * 8 + 8, :]
        if b >= 4:
            part = pltpu.roll(part, NS, 1)
        diag = jnp.where(lane_i == rows_i + 8 * b, part, 0.0)
        on_rows.append(jnp.broadcast_to(jnp.sum(diag, axis=1, keepdims=True), full))
        on_lanes = on_lanes + diag
        w.append(part)
    on_lanes = jnp.broadcast_to(jnp.sum(on_lanes, axis=0, keepdims=True), full)
    on_lanes = jnp.where(left, on_lanes, pltpu.roll(on_lanes, NS, 1))
    unit = rsqrt(on_lanes)
    undo = jnp.where(left, on_lanes * unit, unit)
    for b in range(8):
        eye = (lane_i == rows_i + (NS + 8 * b)).astype(F32)
        w[b] = jnp.where(left, w[b] * (rsqrt(on_rows[b]) * unit), eye)
    out = []
    for b in range(8):
        r = [jnp.broadcast_to(w[b][i : i + 1, :], full) for i in range(8)]
        column = lambda u, i: jnp.broadcast_to(u[:, 8 * b + i : 8 * b + i + 1], full)
        d = {(i, j): column(r[i], j) for i in range(8) for j in range(i, 8)}
        cols = {g: [column(w[g], i) for i in range(8)] for g in range(b + 1, 8)}
        done = []
        for i in range(0, 8, 2):
            k = i + 1
            d00, d01, d11 = d[i, i], d[i, k], d[k, k]
            det = d00 * d11 - d01 * d01
            inv = reciprocal(det)
            a00, a01, a11 = d11 * inv, d01 * inv, d00 * inv
            y = {}
            for j in range(i + 2, 8):
                y[j] = (a00 * d[i, j] - a01 * d[k, j], a11 * d[k, j] - a01 * d[i, j])
            x0 = a00 * r[i] - a01 * r[k]
            x1 = a11 * r[k] - a01 * r[i]
            for j in range(i + 2, 8):
                for m in range(j, 8):
                    d[j, m] = d[j, m] - (d[i, j] * y[m][0] + d[k, j] * y[m][1])
                r[j] = r[j] - (d[i, j] * x0 + d[k, j] * x1)
            for g in range(b + 1, 8):
                c = cols[g]
                w[g] = w[g] - (c[i] * x0 + c[k] * x1)
                for j in range(i + 2, 8):
                    c[j] = c[j] - (c[i] * y[j][0] + c[k] * y[j][1])
            done.append(r[i] * rsqrt(d00))
            done.append((d00 * r[k] - d01 * r[i]) * rsqrt(d00 * det))
        rows = done[0]
        for s in range(1, 8):
            rows = jnp.where(rows_i == s, done[s], rows)
        out.append(rows * undo)
    return jnp.concatenate(out, axis=0)


CHUNKS = 8


def basis_kernel(root, gram, snap, basis, factor, out, out_sem):
    per = 2 * NZ // CHUNKS
    rows = eliminate(gram)
    upper = lax.broadcasted_iota(jnp.int32, (NS, NS), 1) >= lax.broadcasted_iota(jnp.int32, (NS, NS), 0)
    factor[...] = jnp.where(upper, rows[:, :NS] * (1.0 / root), 0.0)
    high, low = split(rows[:, NS:] * root)
    lhs = jnp.concatenate([high, high, low], axis=1)
    stores = []
    for i in range(CHUNKS):
        for k in range(i * per, i * per + per):
            both = snap[k]
            rhs = jnp.concatenate([both, both[:NS]], axis=0)
            res = jnp.dot(lhs, rhs, preferred_element_type=F32)
            for h in range(2):
                out[h, i, pl.ds(k - i * per, NS, stride=8), :] = res[:, h * 128 : h * 128 + 128]
        ph, z0 = divmod(i * per, NZ)
        for h in range(2):
            copy = pltpu.make_async_copy(
                out.at[h, i].reshape(NS, 8, 128),
                basis.at[:, ph, pl.ds(z0, per), pl.ds(h * 128, 128)], out_sem.at[h, i])
            copy.start()
            stores.append(copy)
    for copy in stores:
        copy.wait()


def basis_call(total_rows, gram, snap):
    vm, dma = pltpu.VMEM, pltpu.SemaphoreType.DMA
    anywhere = pl.BlockSpec(memory_space=pl.ANY)
    invmem = pl.BlockSpec(memory_space=pltpu.VMEM)
    root = float(total_rows) ** 0.5
    return pl.pallas_call(
        functools.partial(basis_kernel, root),
        out_shape=(
            jax.ShapeDtypeStruct((NS, 2, NZ, NT), F32),
            jax.ShapeDtypeStruct((NS, NS), F32),
        ),
        in_specs=[invmem, invmem],
        out_specs=(anywhere, invmem),
        scratch_shapes=[
            vm((2, CHUNKS, NS * 8, 128), F32),
            dma((2, CHUNKS)),
        ],
        name="basis",
        compiler_params=pltpu.CompilerParams(vmem_limit_bytes=40 << 20),
    )(gram, snap)


def per_device(total_rows, solid_start, inlet, ntu, solid_rate):
    vm, dma = pltpu.VMEM, pltpu.SemaphoreType.DMA
    anywhere = pl.BlockSpec(memory_space=pl.ANY)
    invmem = pl.BlockSpec(memory_space=pltpu.VMEM)
    gram, snap = pl.pallas_call(
        sweep_kernel,
        out_shape=(
            jax.ShapeDtypeStruct((32, 128), F32),
            jax.ShapeDtypeStruct((2 * NZ, 2 * NS, NT), BF16),
        ),
        in_specs=[pl.BlockSpec(memory_space=pltpu.HBM)] * 4,
        out_specs=(invmem, invmem),
        scratch_shapes=[
            vm((NS, NZ, NT), BF16),
            vm((NZ, NT), F32),
            vm((NZ, NT), F32),
            vm((NS, NT), F32),
            vm((2, NZ // 8, NS * 8, 128), F32),
            vm((7, NZ // 8, 8, NT), F32),
            vm((2 * NZ, NS, NT), F32),
            vm((4, NS, NT), F32),
            vm((2, 8, 128), F32),
            vm((2, LZ, SLICE, 128), F32),
            vm((2, SLICE, 128), F32),
            vm((LZ, SLICE, 128), F32),
            vm((32, 128), F32),
            vm((2, 2, 16, 128), F32),
            vm((LZ, 8, 128), F32),
            vm((2, LZ, SLICE, 128), F32),
            vm((2, LX, SLICE, 128), F32),
            vm((LZ, SLICE, 128), F32),
            vm((2 * LX, 32, 128), F32),
            vm((2, 2, 8, 16, 128), F32),
            vm((128, 64), F32),
            vm((LZ, SLICE, 128), F32),
            dma((4,)),
            dma((12,)),
            dma((12,)),
        ],
        name="sweep",
        compiler_params=pltpu.CompilerParams(
            collective_id=0, has_side_effects=True, vmem_limit_bytes=40 << 20),
    )(*(pltpu.with_memory_space_constraint(v, pltpu.HBM) for v in (solid_start, inlet, ntu, solid_rate)))
    basis, factor = basis_call(total_rows, gram, snap)
    return basis, factor


def solution(mesh):
    placed = (P(None, "ax", "tr"), P(None, "tr"), P("ax", "tr"), P("ax", "tr"))
    total_rows = 2 * NZ * mesh.shape["ax"] * NT * mesh.shape["tr"]
    return jax.shard_map(
        functools.partial(per_device, total_rows),
        mesh=mesh,
        in_specs=placed,
        out_specs=(P(None, None, "ax", "tr"), P()),
        check_vma=False,
    )
```

```python
import functools

import jax
import jax.numpy as jnp
from jax import lax
from jax.experimental import pallas as pl
from jax.experimental.pallas import tpu as pltpu
from jax.sharding import PartitionSpec as P

MESH = pl.DeviceIdType.MESH
F32 = jnp.float32
BF16 = jnp.bfloat16
NS = 64
NZ = 32
NT = 256
LZ, LX, LY = 8, 4, 8
SLICE = NT // LZ


def split(value):
    high = value.astype(BF16)
    low = (value - high.astype(F32)).astype(BF16)
    return high, low


def place():
    ax, tr = lax.axis_index("ax"), lax.axis_index("tr")
    return ax // LZ, lax.rem(ax, LZ), tr // 2, lax.rem(tr, 2)


def device(x, z, y, c):
    return {"ax": x * LZ + z, "tr": y * 2 + c}


def ring(count, body):
    def step(j, carry):
        away = (j + 1) // 2
        body(count // 2 + away * (1 - 2 * lax.rem(j + 1, 2)))
        return carry

    lax.fori_loop(0, count - 1, step, 0)


def await_bytes(ref, sem):
    pltpu.make_async_copy(ref, ref, sem).wait()


def sweep_kernel(
    solid, inlet, ntu, rate,
    gram_out, snap,
    xb, ntu_v, rate_v, inlet_v, xs, coef, snap0, ends,
    send_c, send_bu, send_x, send_e, send_g, send_h, send_d,
    recv_c, recv_bu, recv_x, recv_e, recv_g, recv_h, recv_d,
    coef_t, inlet_t, load_sem, ssem, rsem,
):
    x, z, y, c = place()
    xc = x * 2 + c

    loads = [
        pltpu.make_async_copy(src, dst, load_sem.at[i])
        for i, (src, dst) in enumerate(
            [(ntu, ntu_v), (rate, rate_v), (solid, xb), (inlet, inlet_v)]
        )
    ]
    def peer_z(i):
        return lax.rem(z + i, LZ)

    def peer_y(i):
        return lax.rem(y + i, LY)

    def peer_xc(i):
        return lax.rem(xc + i, 2 * LX)

    def dev_z(i):
        return device(x, peer_z(i), y, c)

    def dev_y(i):
        return device(x, z, peer_y(i), c)

    def dev_xc(i):
        p = peer_xc(i)
        return device(p // 2, z, y, lax.rem(p, 2))

    barrier = pltpu.get_barrier_semaphore()
    for at, (count, dev) in enumerate(((LZ, dev_z), (2 * LX, dev_xc), (LY, dev_y))):
        if at == 1:
            for load in loads:
                load.start()
        ring(count, lambda i, dev=dev: pl.semaphore_signal(
            barrier, inc=1, device_id=dev(i), device_id_type=MESH))

    loads[0].wait()
    loads[1].wait()
    n_all = ntu_v[...]
    r_all = rate_v[...]
    a_all = 1.0 / (1.0 + n_all)
    s_all = n_all * a_all
    sr_all = s_all * r_all
    row = lax.broadcasted_iota(jnp.int32, (8, NT), 0)
    shift = lambda u, k, fill: jnp.where(row >= k, pltpu.roll(u, k, 0), fill)
    groups = range(NZ // 8)
    scales = [[a_all[g * 8 : g * 8 + 8]] for g in groups]
    for k in (1, 2, 4):
        for scale in scales:
            scale.append(scale[-1] * shift(scale[-1], k, 1.0))
    p_all, q_all = [], []
    for g in groups:
        p_all.append(scales[g][3] * p_all[-1][7:8] if g else scales[g][3])
        q = sr_all[g * 8 : g * 8 + 8] * p_all[g]
        for step, k in enumerate((1, 2, 4)):
            q = q + scales[g][step] * shift(q, k, 0.0)
        q_all.append(q)
    for g in groups[1:]:
        q_all[g] = q_all[g] + scales[g][3] * q_all[g - 1][7:8]
    p, q = p_all[-1][7:8], q_all[-1][7:8]
    p_all, q_all = jnp.concatenate(p_all, axis=0), jnp.concatenate(q_all, axis=0)
    for m, u in enumerate((a_all, s_all, p_all, q_all)):
        coef[m] = u.reshape(NZ // 8, 8, NT)
    coef[6] = r_all.reshape(NZ // 8, 8, NT)
    bw = r_all * p_all
    aw = (1.0 - r_all) * bw + r_all * q_all
    coef[4] = bw.reshape(NZ // 8, 8, NT)
    coef[5] = aw.reshape(NZ // 8, 8, NT)
    both = lambda u: jnp.sum(u, axis=0, keepdims=True)
    rows = jnp.concatenate(
        [
            p, q,
            0.5 * both(q_all * q_all + aw * aw),
            both(q_all * p_all + aw * bw),
            0.5 * both(p_all * p_all + bw * bw),
            jnp.zeros((3, NT), F32),
        ],
        axis=0,
    )
    send_c[0] = rows[:, :128]
    send_c[1] = rows[:, 128:]

    loads[2].wait()
    chunk = 16

    def widen(i, carry):
        part = xb[pl.ds(i * 8, 8)].astype(F32)
        for h in range(2):
            for g in range(NZ // 8):
                tile = part[:, g * 8 : g * 8 + 8, h * 128 : h * 128 + 128]
                xs[h, g, pl.ds(pl.multiple_of(i * 64, 64), 64), :] = tile.reshape(64, 128)
        return carry

    lax.fori_loop(0, NS // 8, widen, 0)

    def sweep_chunk(ci, carry):
        n0 = ci * chunk

        def plane(kg, i, state):
            new = []
            k = kg * 8 + i
            for h in range(2):
                f1, f2, u1, u2 = state[h]
                lanes = pl.ds(h * 128, 128)
                one = lambda m: jnp.broadcast_to(coef[m, kg, i : i + 1, lanes], (chunk, 128))
                a, s, pp, qq, bb, aa, r = (one(m) for m in range(7))
                v = xs[h, kg, pl.ds(n0 * 8 + i, chunk, stride=8), :]
                f1 = a * f1 + s * v
                v = v + r * (f1 - v)
                f2 = a * f2 + s * v
                w = v + r * (f2 - v)
                snap0[k, pl.ds(n0, chunk), lanes] = f2
                snap0[NZ + k, pl.ds(n0, chunk), lanes] = w
                u1 = u1 + (qq * f2 + aa * w)
                u2 = u2 + (pp * f2 + bb * w)
                new.append((f1, f2, u1, u2))
            return tuple(new)

        def planes(kg, state):
            for i in range(8):
                state = plane(kg, i, state)
            return state

        zero = jnp.zeros((chunk, 128), F32)
        state = lax.fori_loop(0, NZ // 8, planes, ((zero,) * 4,) * 2)
        for h in range(2):
            for m in range(4):
                ends[m, pl.ds(n0, chunk), h * 128 : h * 128 + 128] = state[h][m]
        return carry

    lax.fori_loop(0, NS // chunk, sweep_chunk, 0)
    for m in range(2):
        flat = jnp.concatenate([ends[2 * m], ends[2 * m + 1]], axis=0)
        send_bu[m] = flat.T.reshape(LZ, SLICE, 128)

    pl.semaphore_wait(barrier, (LZ - 1) + (2 * LX - 1) + (LY - 1))

    ring(LZ, lambda i: pltpu.make_async_remote_copy(
        send_c.at[peer_z(i) // 4], recv_c.at[z], ssem.at[0], rsem.at[0],
        device_id=dev_z(i), device_id_type=MESH).start())
    for m in (0,):
        ring(LZ, lambda i: pltpu.make_async_remote_copy(
            send_bu.at[m, peer_z(i)], recv_bu.at[m, z], ssem.at[1 + m], rsem.at[1 + m],
            device_id=dev_z(i), device_id_type=MESH).start())
    recv_c[z] = send_c[z // 4]
    recv_bu[0, z] = send_bu[0, z]
    recv_bu[1, z] = send_bu[1, z]

    loads[3].wait()
    inl = inlet_v[...]
    inlet_t[...] = jnp.concatenate([inl, inl], axis=0).T.reshape(LZ, SLICE, 128)

    def inner(k, acc):
        high, low = split(snap0[k])
        rowsb = jnp.concatenate([high, low], axis=0)
        return acc + lax.dot_general(rowsb, rowsb, (((1,), (1,)), ((), ())), preferred_element_type=F32)

    acc = lax.fori_loop(0, 2 * NZ, inner, jnp.zeros((2 * NS, 2 * NS), F32), unroll=4)
    for m in (1,):
        ring(LZ, lambda i: pltpu.make_async_remote_copy(
            send_bu.at[m, peer_z(i)], recv_bu.at[m, z], ssem.at[1 + m], rsem.at[1 + m],
            device_id=dev_z(i), device_id_type=MESH).start())
    gram0 = (acc[:NS, :NS] + acc[NS:, NS:]) + (acc[:NS, NS:] + acc[NS:, :NS])

    await_bytes(recv_c.at[pl.ds(0, LZ - 1)], rsem.at[0])
    coef_t[...] = recv_c[...].reshape(LZ * 8, 128).T
    ct = coef_t[pl.ds(pl.multiple_of(lax.rem(z, 4) * SLICE, SLICE), SLICE), :]
    lane = lax.broadcasted_iota(jnp.int32, (SLICE, 128), 1)
    second = lane >= NS
    wide = lambda k, m: jnp.broadcast_to(ct[:, k * 8 + m : k * 8 + m + 1], (SLICE, 128))
    turn = lambda u: pltpu.roll(u, NS, 1)
    first = lambda u: jnp.where(second, 0.0, u)
    aks = [wide(k, 0) for k in range(LZ)]
    cks = [wide(k, 1) for k in range(LZ)]
    c2s = [jnp.where(second, ck, 0.0) for ck in cks]
    at, ctot = aks[0], cks[0]
    reach = [None]
    for k in range(1, LZ):
        reach.append((at, ctot))
        at, ctot = aks[k] * at, aks[k] * ctot + cks[k] * at
    send_x[1] = jnp.where(second, ctot, at)

    def send_line(part):
        def send(i):
            px = lax.rem(x + i, LX)
            pltpu.make_async_remote_copy(
                send_x.at[part], recv_x.at[part, x], ssem.at[3 + 8 * part], rsem.at[3 + 8 * part],
                device_id=device(px, z, y, c), device_id_type=MESH).start()

        ring(LX, send)
        recv_x[part, x] = send_x[part]

    send_line(1)
    await_bytes(recv_bu.at[0, pl.ds(0, LZ - 1)], rsem.at[1])
    bks = [recv_bu[0, k] for k in range(LZ)]
    bds = [jnp.where(second, turn(b), b) for b in bks]
    full, dup = bks[0], bds[0]
    before = [None]
    for k in range(1, LZ):
        before.append((full,) + reach[k])
        full, dup = aks[k] * full + c2s[k] * dup + bks[k], aks[k] * dup + bds[k]
    send_x[0] = full
    send_line(0)

    aas, abs_, bbs = ([wide(k, m) for k in range(LZ)] for m in (2, 3, 4))
    aa, ab, bb = aas[0], abs_[0], bbs[0]
    for k in range(1, LZ):
        _, ah, ch = before[k]
        a2 = ah * ah
        ac = ah * ch
        aa = aa + (aas[k] * a2 + abs_[k] * ac + bbs[k] * (ch * ch))
        ab = ab + (abs_[k] * a2 + 2.0 * bbs[k] * ac)
        bb = bb + bbs[k] * a2
    await_bytes(recv_bu.at[1, pl.ds(0, LZ - 1)], rsem.at[2])
    answer = recv_bu[1, 0]
    vs = []
    for k in range(1, LZ):
        e0, ah, ch = before[k]
        te = turn(e0)
        own = jnp.where(second, bbs[k], aas[k]) * e0
        u = recv_bu[1, k]
        vs.append(u + own + first(abs_[k]) * te)
        w = u + 2.0 * own + abs_[k] * te
        answer = answer + (ah * w + first(ch) * turn(w))

    def cross(v, e):
        vh, vl = split(v)
        eh, el = split(e)
        prod = lax.dot_general(
            jnp.concatenate([vh, vl], axis=1), jnp.concatenate([eh, el], axis=1),
            (((0,), (0,)), ((), ())), preferred_element_type=F32)
        prod = (prod[:128, :128] + prod[128:, 128:]) + (prod[:128, 128:] + prod[128:, :128])
        part = prod[:NS, :NS] + prod[NS:, NS:]
        return part + part.T

    gram1 = gram0 + cross(
        jnp.concatenate(vs, axis=0), jnp.concatenate([before[k][0] for k in range(1, LZ)], axis=0))
    for part in range(2):
        await_bytes(recv_x.at[part, pl.ds(0, LX - 1)], rsem.at[3 + 8 * part])
    e = inlet_t[z]
    d = e
    for k in range(LX - 1):
        f, cf = recv_x[0, k], recv_x[1, k]
        rolled = turn(cf)
        a = jnp.where(second, rolled, cf)
        c2 = jnp.where(second, cf, 0.0)
        fd = jnp.where(second, turn(f), f)
        e_new = a * e + c2 * d + f
        d_new = a * d + fd
        upstream = jnp.full((SLICE, 128), k, jnp.int32) < x
        e = jnp.where(upstream, e_new, e)
        d = jnp.where(upstream, d_new, d)
    gram = gram1 + cross(answer + jnp.where(second, bb, aa) * e + first(ab) * turn(e), e)
    half = NS // 2
    down = lax.broadcasted_iota(jnp.int32, (half, half), 0)
    over = lax.broadcasted_iota(jnp.int32, (half, half), 1)
    far = gram[half:, half:]
    square = jnp.concatenate([jnp.where(over >= down, gram[:half, :half], far), gram[:half, half:]], axis=1)
    send_g[...] = jnp.concatenate([square[:16], square[16:]], axis=1)
    diag = jnp.sum(jnp.where(over == down, far, 0.0), axis=0, keepdims=True)
    send_d[0] = jnp.concatenate([diag, jnp.zeros((1, 128 - half), F32)], axis=1)

    def send_sum(i):
        for src, dst, slot in ((send_g, recv_g.at[xc], 5), (send_d.at[0], recv_d.at[0, xc], 10)):
            pltpu.make_async_remote_copy(
                src, dst, ssem.at[slot], rsem.at[slot], device_id=dev_xc(i), device_id_type=MESH).start()

    ring(2 * LX, send_sum)

    for k in range(LZ):
        send_e[k] = e
        if k < LZ - 1:
            e, d = aks[k] * e + c2s[k] * d + bks[k], aks[k] * d + bds[k]
    ring(LZ, lambda i: pltpu.make_async_remote_copy(
        send_e.at[peer_z(i)], recv_e.at[z], ssem.at[4], rsem.at[4],
        device_id=dev_z(i), device_id_type=MESH).start())
    recv_e[z] = send_e[z]
    recv_g[xc] = send_g[...]
    recv_d[0, xc] = send_d[0]
    await_bytes(recv_g.at[pl.ds(0, 2 * LX - 1)], rsem.at[5])
    await_bytes(recv_d.at[0, pl.ds(0, 7)], rsem.at[10])

    def add(parts):
        while len(parts) > 1:
            parts = [parts[i] + parts[i + 1] for i in range(0, len(parts), 2)]
        return parts[0]

    sums = add([recv_g[i] for i in range(2 * LX)])
    halves = [sums[:8], sums[8:], add([recv_d[0, i] for i in range(2 * LX)])]
    for phase in range(2):
        for h in range(2):
            send_h[phase, h] = halves[h]
        send_d[1 + phase] = halves[2]
        def send_halves(i):
            for h in range(2):
                over_z = (h + phase) % 2 == 0
                dev, mine, slot = dev_z(i) if over_z else dev_y(i), z if over_z else y, 6 + 2 * phase + h
                pltpu.make_async_remote_copy(
                    send_h.at[phase, h], recv_h.at[phase, h, mine], ssem.at[slot], rsem.at[slot],
                    device_id=dev, device_id_type=MESH).start()
            dev, mine = (dev_y(i), y) if phase else (dev_z(i), z)
            pltpu.make_async_remote_copy(
                send_d.at[1 + phase], recv_d.at[1 + phase, mine], ssem.at[12 + phase], rsem.at[12 + phase],
                device_id=dev, device_id_type=MESH).start()

        ring(8, send_halves)
        recv_d[1 + phase, y if phase else z] = halves[2]
        for h in range(2):
            recv_h[phase, h, z if (h + phase) % 2 == 0 else y] = halves[h]
        if phase == 1:
            await_bytes(recv_e.at[pl.ds(0, LZ - 1)], rsem.at[4])
            ends_t = recv_e[...].reshape(NT, 128).T
            ends[0] = ends_t[:NS]
            ends[1] = ends_t[NS:]

            def finish(kg, carry):
                for i in range(8):
                    k = kg * 8 + i
                    for ph, m1, m2 in ((0, 3, 2), (1, 5, 4)):
                        c1 = coef[m1, kg, i : i + 1, :]
                        c2_ = coef[m2, kg, i : i + 1, :]
                        high, low = split(snap0[ph * NZ + k] + c1 * ends[0] + c2_ * ends[1])
                        snap[ph * NZ + k, :NS, :] = high
                        snap[ph * NZ + k, NS:, :] = low
                return carry

            lax.fori_loop(0, NZ // 8, finish, 0)
        for h in range(2):
            slot = 6 + 2 * phase + h
            await_bytes(recv_h.at[phase, h, pl.ds(0, 7)], rsem.at[slot])
        await_bytes(recv_d.at[1 + phase, pl.ds(0, 7)], rsem.at[12 + phase])
        halves = [add([recv_h[phase, h, i] for i in range(8)]) for h in range(2)]
        halves.append(add([recv_d[1 + phase, i] for i in range(8)]))
    square = jnp.concatenate(halves[:2], axis=0)
    square = jnp.concatenate([square[:, :NS], square[:, NS:]], axis=0)
    near, side = square[:, :half], square[:, half:]
    flip = near.T
    far = jnp.where(over < down, near, jnp.where(over == down, halves[2][:, :half], flip))
    gram_out[...] = jnp.concatenate([jnp.where(over >= down, near, flip), side, side.T, far], axis=1)

    await_bytes(recv_c.at[pl.ds(0, LZ - 1)], ssem.at[0])
    await_bytes(recv_bu.at[0, pl.ds(0, LZ - 1)], ssem.at[1])
    await_bytes(recv_bu.at[1, pl.ds(0, LZ - 1)], ssem.at[2])
    for part in range(2):
        await_bytes(recv_x.at[part, pl.ds(0, LX - 1)], ssem.at[3 + 8 * part])
    await_bytes(recv_e.at[pl.ds(0, LZ - 1)], ssem.at[4])
    await_bytes(recv_g.at[pl.ds(0, 2 * LX - 1)], ssem.at[5])
    for slot in (10, 12, 13):
        await_bytes(recv_d.at[0, pl.ds(0, 7)], ssem.at[slot])
    for slot in range(6, 10):
        await_bytes(recv_h.at[0, 0, pl.ds(0, 7)], ssem.at[slot])


def reciprocal(d):
    r = pl.reciprocal(d, approx=True)
    return r * (2.0 - d * r)


def rsqrt(d):
    r = lax.rsqrt(d)
    return r * (1.5 - (0.5 * d * r) * r)


def eliminate(gram):
    full = (8, 128)
    rows_i = lax.broadcasted_iota(jnp.int32, full, 0)
    lane_i = lax.broadcasted_iota(jnp.int32, full, 1)
    left = lane_i < NS
    w, on_rows, on_lanes = [], [], jnp.zeros(full, F32)
    for b in range(8):
        part = gram[(b % 4) * 8 : (b % 4) * 8 + 8, :]
        if b >= 4:
            part = pltpu.roll(part, NS, 1)
        diag = jnp.where(lane_i == rows_i + 8 * b, part, 0.0)
        on_rows.append(jnp.broadcast_to(jnp.sum(diag, axis=1, keepdims=True), full))
        on_lanes = on_lanes + diag
        w.append(part)
    on_lanes = jnp.broadcast_to(jnp.sum(on_lanes, axis=0, keepdims=True), full)
    on_lanes = jnp.where(left, on_lanes, pltpu.roll(on_lanes, NS, 1))
    unit = rsqrt(on_lanes)
    undo = jnp.where(left, on_lanes * unit, unit)
    for b in range(8):
        eye = (lane_i == rows_i + (NS + 8 * b)).astype(F32)
        w[b] = jnp.where(left, w[b] * (rsqrt(on_rows[b]) * unit), eye)
    out = []
    for b in range(8):
        r = [jnp.broadcast_to(w[b][i : i + 1, :], full) for i in range(8)]
        column = lambda u, i: jnp.broadcast_to(u[:, 8 * b + i : 8 * b + i + 1], full)
        d = {(i, j): column(r[i], j) for i in range(8) for j in range(i, 8)}
        cols = {g: [column(w[g], i) for i in range(8)] for g in range(b + 1, 8)}
        done = []
        for i in range(0, 8, 2):
            k = i + 1
            d00, d01, d11 = d[i, i], d[i, k], d[k, k]
            det = d00 * d11 - d01 * d01
            inv = reciprocal(det)
            a00, a01, a11 = d11 * inv, d01 * inv, d00 * inv
            y = {}
            for j in range(i + 2, 8):
                y[j] = (a00 * d[i, j] - a01 * d[k, j], a11 * d[k, j] - a01 * d[i, j])
            x0 = a00 * r[i] - a01 * r[k]
            x1 = a11 * r[k] - a01 * r[i]
            for j in range(i + 2, 8):
                for m in range(j, 8):
                    d[j, m] = d[j, m] - (d[i, j] * y[m][0] + d[k, j] * y[m][1])
                r[j] = r[j] - (d[i, j] * x0 + d[k, j] * x1)
            for g in range(b + 1, 8):
                c = cols[g]
                w[g] = w[g] - (c[i] * x0 + c[k] * x1)
                for j in range(i + 2, 8):
                    c[j] = c[j] - (c[i] * y[j][0] + c[k] * y[j][1])
            done.append(r[i] * rsqrt(d00))
            done.append((d00 * r[k] - d01 * r[i]) * rsqrt(d00 * det))
        rows = done[0]
        for s in range(1, 8):
            rows = jnp.where(rows_i == s, done[s], rows)
        out.append(rows * undo)
    return jnp.concatenate(out, axis=0)


CHUNKS = 8


def basis_kernel(root, gram, snap, basis, factor, out, out_sem):
    per = 2 * NZ // CHUNKS
    rows = eliminate(gram)
    upper = lax.broadcasted_iota(jnp.int32, (NS, NS), 1) >= lax.broadcasted_iota(jnp.int32, (NS, NS), 0)
    factor[...] = jnp.where(upper, rows[:, :NS] * (1.0 / root), 0.0)
    high, low = split(rows[:, NS:] * root)
    lhs = jnp.concatenate([high, high, low], axis=1)
    stores = []
    for i in range(CHUNKS):
        for k in range(i * per, i * per + per):
            both = snap[k]
            rhs = jnp.concatenate([both, both[:NS]], axis=0)
            res = jnp.dot(lhs, rhs, preferred_element_type=F32)
            for h in range(2):
                out[h, i, pl.ds(k - i * per, NS, stride=8), :] = res[:, h * 128 : h * 128 + 128]
        ph, z0 = divmod(i * per, NZ)
        for h in range(2):
            copy = pltpu.make_async_copy(
                out.at[h, i].reshape(NS, 8, 128),
                basis.at[:, ph, pl.ds(z0, per), pl.ds(h * 128, 128)], out_sem.at[h, i])
            copy.start()
            stores.append(copy)
    for copy in stores:
        copy.wait()


def basis_call(total_rows, gram, snap):
    vm, dma = pltpu.VMEM, pltpu.SemaphoreType.DMA
    anywhere = pl.BlockSpec(memory_space=pl.ANY)
    invmem = pl.BlockSpec(memory_space=pltpu.VMEM)
    root = float(total_rows) ** 0.5
    return pl.pallas_call(
        functools.partial(basis_kernel, root),
        out_shape=(
            jax.ShapeDtypeStruct((NS, 2, NZ, NT), F32),
            jax.ShapeDtypeStruct((NS, NS), F32),
        ),
        in_specs=[invmem, invmem],
        out_specs=(anywhere, invmem),
        scratch_shapes=[
            vm((2, CHUNKS, NS * 8, 128), F32),
            dma((2, CHUNKS)),
        ],
        name="basis",
        compiler_params=pltpu.CompilerParams(vmem_limit_bytes=40 << 20),
    )(gram, snap)


def per_device(total_rows, solid_start, inlet, ntu, solid_rate):
    vm, dma = pltpu.VMEM, pltpu.SemaphoreType.DMA
    anywhere = pl.BlockSpec(memory_space=pl.ANY)
    invmem = pl.BlockSpec(memory_space=pltpu.VMEM)
    gram, snap = pl.pallas_call(
        sweep_kernel,
        out_shape=(
            jax.ShapeDtypeStruct((32, 128), F32),
            jax.ShapeDtypeStruct((2 * NZ, 2 * NS, NT), BF16),
        ),
        in_specs=[pl.BlockSpec(memory_space=pltpu.HBM)] * 4,
        out_specs=(invmem, invmem),
        scratch_shapes=[
            vm((NS, NZ, NT), BF16),
            vm((NZ, NT), F32),
            vm((NZ, NT), F32),
            vm((NS, NT), F32),
            vm((2, NZ // 8, NS * 8, 128), F32),
            vm((7, NZ // 8, 8, NT), F32),
            vm((2 * NZ, NS, NT), F32),
            vm((4, NS, NT), F32),
            vm((2, 8, 128), F32),
            vm((2, LZ, SLICE, 128), F32),
            vm((2, SLICE, 128), F32),
            vm((LZ, SLICE, 128), F32),
            vm((16, 128), F32),
            vm((2, 2, 8, 128), F32),
            vm((3, 1, 128), F32),
            vm((LZ, 8, 128), F32),
            vm((2, LZ, SLICE, 128), F32),
            vm((2, LX, SLICE, 128), F32),
            vm((LZ, SLICE, 128), F32),
            vm((2 * LX, 16, 128), F32),
            vm((2, 2, 8, 8, 128), F32),
            vm((3, 8, 1, 128), F32),
            vm((128, 64), F32),
            vm((LZ, SLICE, 128), F32),
            dma((4,)),
            dma((14,)),
            dma((14,)),
        ],
        name="sweep",
        compiler_params=pltpu.CompilerParams(
            collective_id=0, has_side_effects=True, vmem_limit_bytes=40 << 20),
    )(*(pltpu.with_memory_space_constraint(v, pltpu.HBM) for v in (solid_start, inlet, ntu, solid_rate)))
    basis, factor = basis_call(total_rows, gram, snap)
    return basis, factor


def solution(mesh):
    placed = (P(None, "ax", "tr"), P(None, "tr"), P("ax", "tr"), P("ax", "tr"))
    total_rows = 2 * NZ * mesh.shape["ax"] * NT * mesh.shape["tr"]
    return jax.shard_map(
        functools.partial(per_device, total_rows),
        mesh=mesh,
        in_specs=placed,
        out_specs=(P(None, None, "ax", "tr"), P()),
        check_vma=False,
    )
```

```python
import functools

import jax
import jax.numpy as jnp
from jax import lax
from jax.experimental import pallas as pl
from jax.experimental.pallas import tpu as pltpu
from jax.sharding import PartitionSpec as P

MESH = pl.DeviceIdType.MESH
F32 = jnp.float32
BF16 = jnp.bfloat16
NS = 64
NZ = 32
NT = 256
LZ, LX, LY = 8, 4, 8
SLICE = NT // LZ


def split(value):
    high = value.astype(BF16)
    low = (value - high.astype(F32)).astype(BF16)
    return high, low


def place():
    ax, tr = lax.axis_index("ax"), lax.axis_index("tr")
    return ax // LZ, lax.rem(ax, LZ), tr // 2, lax.rem(tr, 2)


def device(x, z, y, c):
    return {"ax": x * LZ + z, "tr": y * 2 + c}


def ring(count, body):
    def step(j, carry):
        away = (j + 1) // 2
        body(count // 2 + away * (1 - 2 * lax.rem(j + 1, 2)))
        return carry

    lax.fori_loop(0, count - 1, step, 0)


def await_bytes(ref, sem):
    pltpu.make_async_copy(ref, ref, sem).wait()


def sweep_kernel(
    solid, inlet, ntu, rate,
    gram_out, snap,
    xb, ntu_v, rate_v, inlet_v, xs, coef, snap0, ends,
    send_c, send_bu, send_x, send_e, send_g, send_h, send_d,
    recv_c, recv_bu, recv_x, recv_e, recv_g, recv_h, recv_d,
    coef_t, inlet_t, load_sem, ssem, rsem,
):
    x, z, y, c = place()
    xc = x * 2 + c

    loads = [
        pltpu.make_async_copy(src, dst, load_sem.at[i])
        for i, (src, dst) in enumerate(
            [(ntu, ntu_v), (rate, rate_v), (solid, xb), (inlet, inlet_v)]
        )
    ]
    def peer_z(i):
        return lax.rem(z + i, LZ)

    def peer_y(i):
        return lax.rem(y + i, LY)

    def peer_xc(i):
        return lax.rem(xc + i, 2 * LX)

    def dev_z(i):
        return device(x, peer_z(i), y, c)

    def dev_y(i):
        return device(x, z, peer_y(i), c)

    def dev_xc(i):
        p = peer_xc(i)
        return device(p // 2, z, y, lax.rem(p, 2))

    barrier = pltpu.get_barrier_semaphore()
    for at, (count, dev) in enumerate(((LZ, dev_z), (2 * LX, dev_xc), (LY, dev_y))):
        if at == 1:
            for load in loads:
                load.start()
        ring(count, lambda i, dev=dev: pl.semaphore_signal(
            barrier, inc=1, device_id=dev(i), device_id_type=MESH))

    loads[0].wait()
    loads[1].wait()
    n_all = ntu_v[...]
    r_all = rate_v[...]
    a_all = 1.0 / (1.0 + n_all)
    s_all = n_all * a_all
    sr_all = s_all * r_all
    row = lax.broadcasted_iota(jnp.int32, (8, NT), 0)
    shift = lambda u, k, fill: jnp.where(row >= k, pltpu.roll(u, k, 0), fill)
    groups = range(NZ // 8)
    scales = [[a_all[g * 8 : g * 8 + 8]] for g in groups]
    for k in (1, 2, 4):
        for scale in scales:
            scale.append(scale[-1] * shift(scale[-1], k, 1.0))
    p_all, q_all = [], []
    for g in groups:
        p_all.append(scales[g][3] * p_all[-1][7:8] if g else scales[g][3])
        q = sr_all[g * 8 : g * 8 + 8] * p_all[g]
        for step, k in enumerate((1, 2, 4)):
            q = q + scales[g][step] * shift(q, k, 0.0)
        q_all.append(q)
    for g in groups[1:]:
        q_all[g] = q_all[g] + scales[g][3] * q_all[g - 1][7:8]
    p, q = p_all[-1][7:8], q_all[-1][7:8]
    p_all, q_all = jnp.concatenate(p_all, axis=0), jnp.concatenate(q_all, axis=0)
    for m, u in enumerate((a_all, s_all, p_all, q_all)):
        coef[m] = u.reshape(NZ // 8, 8, NT)
    coef[6] = r_all.reshape(NZ // 8, 8, NT)
    bw = r_all * p_all
    aw = (1.0 - r_all) * bw + r_all * q_all
    coef[4] = bw.reshape(NZ // 8, 8, NT)
    coef[5] = aw.reshape(NZ // 8, 8, NT)
    both = lambda u: jnp.sum(u, axis=0, keepdims=True)
    rows = jnp.concatenate(
        [
            p, q,
            0.5 * both(q_all * q_all + aw * aw),
            both(q_all * p_all + aw * bw),
            0.5 * both(p_all * p_all + bw * bw),
            jnp.zeros((3, NT), F32),
        ],
        axis=0,
    )
    send_c[0] = rows[:, :128]
    send_c[1] = rows[:, 128:]

    loads[2].wait()
    chunk = 16

    def widen(i, carry):
        part = xb[pl.ds(i * 8, 8)].astype(F32)
        for h in range(2):
            for g in range(NZ // 8):
                tile = part[:, g * 8 : g * 8 + 8, h * 128 : h * 128 + 128]
                xs[h, g, pl.ds(pl.multiple_of(i * 64, 64), 64), :] = tile.reshape(64, 128)
        return carry

    lax.fori_loop(0, NS // 8, widen, 0)

    def sweep_chunk(ci, carry):
        n0 = ci * chunk

        def plane(kg, i, state):
            new = []
            k = kg * 8 + i
            for h in range(2):
                f1, f2, u1, u2 = state[h]
                lanes = pl.ds(h * 128, 128)
                one = lambda m: jnp.broadcast_to(coef[m, kg, i : i + 1, lanes], (chunk, 128))
                a, s, pp, qq, bb, aa, r = (one(m) for m in range(7))
                v = xs[h, kg, pl.ds(n0 * 8 + i, chunk, stride=8), :]
                f1 = a * f1 + s * v
                v = v + r * (f1 - v)
                f2 = a * f2 + s * v
                w = v + r * (f2 - v)
                snap0[k, pl.ds(n0, chunk), lanes] = f2
                snap0[NZ + k, pl.ds(n0, chunk), lanes] = w
                u1 = u1 + (qq * f2 + aa * w)
                u2 = u2 + (pp * f2 + bb * w)
                new.append((f1, f2, u1, u2))
            return tuple(new)

        def planes(kg, state):
            for i in range(8):
                state = plane(kg, i, state)
            return state

        zero = jnp.zeros((chunk, 128), F32)
        state = lax.fori_loop(0, NZ // 8, planes, ((zero,) * 4,) * 2)
        for h in range(2):
            for m in range(4):
                ends[m, pl.ds(n0, chunk), h * 128 : h * 128 + 128] = state[h][m]
        return carry

    lax.fori_loop(0, NS // chunk, sweep_chunk, 0)
    for m in range(2):
        flat = jnp.concatenate([ends[2 * m], ends[2 * m + 1]], axis=0)
        send_bu[m] = flat.T.reshape(LZ, SLICE, 128)

    pl.semaphore_wait(barrier, (LZ - 1) + (2 * LX - 1) + (LY - 1))

    ring(LZ, lambda i: pltpu.make_async_remote_copy(
        send_c.at[peer_z(i) // 4], recv_c.at[z], ssem.at[0], rsem.at[0],
        device_id=dev_z(i), device_id_type=MESH).start())
    for m in (0,):
        ring(LZ, lambda i: pltpu.make_async_remote_copy(
            send_bu.at[m, peer_z(i)], recv_bu.at[m, z], ssem.at[1 + m], rsem.at[1 + m],
            device_id=dev_z(i), device_id_type=MESH).start())
    recv_c[z] = send_c[z // 4]
    recv_bu[0, z] = send_bu[0, z]
    recv_bu[1, z] = send_bu[1, z]

    loads[3].wait()
    inl = inlet_v[...]
    inlet_t[...] = jnp.concatenate([inl, inl], axis=0).T.reshape(LZ, SLICE, 128)

    def inner(k, acc):
        high, low = split(snap0[k])
        rowsb = jnp.concatenate([high, low], axis=0)
        return acc + lax.dot_general(rowsb, rowsb, (((1,), (1,)), ((), ())), preferred_element_type=F32)

    acc = lax.fori_loop(0, 2 * NZ, inner, jnp.zeros((2 * NS, 2 * NS), F32), unroll=4)
    for m in (1,):
        ring(LZ, lambda i: pltpu.make_async_remote_copy(
            send_bu.at[m, peer_z(i)], recv_bu.at[m, z], ssem.at[1 + m], rsem.at[1 + m],
            device_id=dev_z(i), device_id_type=MESH).start())
    gram0 = (acc[:NS, :NS] + acc[NS:, NS:]) + (acc[:NS, NS:] + acc[NS:, :NS])

    await_bytes(recv_c.at[pl.ds(0, LZ - 1)], rsem.at[0])
    coef_t[...] = recv_c[...].reshape(LZ * 8, 128).T
    ct = coef_t[pl.ds(pl.multiple_of(lax.rem(z, 4) * SLICE, SLICE), SLICE), :]
    lane = lax.broadcasted_iota(jnp.int32, (SLICE, 128), 1)
    second = lane >= NS
    wide = lambda k, m: jnp.broadcast_to(ct[:, k * 8 + m : k * 8 + m + 1], (SLICE, 128))
    turn = lambda u: pltpu.roll(u, NS, 1)
    first = lambda u: jnp.where(second, 0.0, u)
    aks = [wide(k, 0) for k in range(LZ)]
    cks = [wide(k, 1) for k in range(LZ)]
    c2s = [jnp.where(second, ck, 0.0) for ck in cks]
    at, ctot = aks[0], cks[0]
    reach = [None]
    for k in range(1, LZ):
        reach.append((at, ctot))
        at, ctot = aks[k] * at, aks[k] * ctot + cks[k] * at
    send_x[1] = jnp.where(second, ctot, at)

    def send_line(part):
        def send(i):
            px = lax.rem(x + i, LX)
            pltpu.make_async_remote_copy(
                send_x.at[part], recv_x.at[part, x], ssem.at[3 + 8 * part], rsem.at[3 + 8 * part],
                device_id=device(px, z, y, c), device_id_type=MESH).start()

        ring(LX, send)
        recv_x[part, x] = send_x[part]

    send_line(1)
    await_bytes(recv_bu.at[0, pl.ds(0, LZ - 1)], rsem.at[1])
    bks = [recv_bu[0, k] for k in range(LZ)]
    bds = [jnp.where(second, turn(b), b) for b in bks]
    full, dup = bks[0], bds[0]
    before = [None]
    for k in range(1, LZ):
        before.append((full,) + reach[k])
        full, dup = aks[k] * full + c2s[k] * dup + bks[k], aks[k] * dup + bds[k]
    send_x[0] = full
    send_line(0)

    aas, abs_, bbs = ([wide(k, m) for k in range(LZ)] for m in (2, 3, 4))
    aa, ab, bb = aas[0], abs_[0], bbs[0]
    for k in range(1, LZ):
        _, ah, ch = before[k]
        a2 = ah * ah
        ac = ah * ch
        aa = aa + (aas[k] * a2 + abs_[k] * ac + bbs[k] * (ch * ch))
        ab = ab + (abs_[k] * a2 + 2.0 * bbs[k] * ac)
        bb = bb + bbs[k] * a2
    await_bytes(recv_bu.at[1, pl.ds(0, LZ - 1)], rsem.at[2])
    answer = recv_bu[1, 0]
    vs = []
    for k in range(1, LZ):
        e0, ah, ch = before[k]
        te = turn(e0)
        own = jnp.where(second, bbs[k], aas[k]) * e0
        u = recv_bu[1, k]
        vs.append(u + own + first(abs_[k]) * te)
        w = u + 2.0 * own + abs_[k] * te
        answer = answer + (ah * w + first(ch) * turn(w))

    def cross(v, e):
        vh, vl = split(v)
        eh, el = split(e)
        prod = lax.dot_general(
            jnp.concatenate([vh, vl], axis=1), jnp.concatenate([eh, el], axis=1),
            (((0,), (0,)), ((), ())), preferred_element_type=F32)
        prod = (prod[:128, :128] + prod[128:, 128:]) + (prod[:128, 128:] + prod[128:, :128])
        part = prod[:NS, :NS] + prod[NS:, NS:]
        return part + part.T

    gram1 = gram0 + cross(
        jnp.concatenate(vs, axis=0), jnp.concatenate([before[k][0] for k in range(1, LZ)], axis=0))
    for part in range(2):
        await_bytes(recv_x.at[part, pl.ds(0, LX - 1)], rsem.at[3 + 8 * part])
    e = inlet_t[z]
    d = e
    for k in range(LX - 1):
        f, cf = recv_x[0, k], recv_x[1, k]
        rolled = turn(cf)
        a = jnp.where(second, rolled, cf)
        c2 = jnp.where(second, cf, 0.0)
        fd = jnp.where(second, turn(f), f)
        e_new = a * e + c2 * d + f
        d_new = a * d + fd
        upstream = jnp.full((SLICE, 128), k, jnp.int32) < x
        e = jnp.where(upstream, e_new, e)
        d = jnp.where(upstream, d_new, d)
    gram = gram1 + cross(answer + jnp.where(second, bb, aa) * e + first(ab) * turn(e), e)
    half = NS // 2
    down = lax.broadcasted_iota(jnp.int32, (half, half), 0)
    over = lax.broadcasted_iota(jnp.int32, (half, half), 1)
    far = gram[half:, half:]
    square = jnp.concatenate([jnp.where(over >= down, gram[:half, :half], far), gram[:half, half:]], axis=1)
    send_g[...] = jnp.concatenate([square[:16], square[16:]], axis=1)
    diag = jnp.sum(jnp.where(over == down, far, 0.0), axis=0, keepdims=True)
    send_d[0] = jnp.concatenate([diag, jnp.zeros((1, 128 - half), F32)], axis=1)

    def send_sum(i):
        for src, dst, slot in ((send_g, recv_g.at[xc], 5), (send_d.at[0], recv_d.at[0, xc], 10)):
            pltpu.make_async_remote_copy(
                src, dst, ssem.at[slot], rsem.at[slot], device_id=dev_xc(i), device_id_type=MESH).start()

    ring(2 * LX, send_sum)

    for k in range(LZ):
        send_e[k] = e
        if k < LZ - 1:
            e, d = aks[k] * e + c2s[k] * d + bks[k], aks[k] * d + bds[k]
    ring(LZ, lambda i: pltpu.make_async_remote_copy(
        send_e.at[peer_z(i)], recv_e.at[z], ssem.at[4], rsem.at[4],
        device_id=dev_z(i), device_id_type=MESH).start())
    recv_e[z] = send_e[z]
    recv_g[xc] = send_g[...]
    recv_d[0, xc] = send_d[0]
    await_bytes(recv_g.at[pl.ds(0, 2 * LX - 1)], rsem.at[5])
    await_bytes(recv_d.at[0, pl.ds(0, 7)], rsem.at[10])

    def add(parts):
        while len(parts) > 1:
            parts = [parts[i] + parts[i + 1] for i in range(0, len(parts), 2)]
        return parts[0]

    sums = add([recv_g[i] for i in range(2 * LX)])
    halves = [sums[:8], sums[8:], add([recv_d[0, i] for i in range(2 * LX)])]
    for phase in range(2):
        for h in range(2):
            send_h[phase, h] = halves[h]
        send_d[1 + phase] = halves[2]
        def send_halves(i):
            for h in range(2):
                over_z = (h + phase) % 2 == 0
                dev, mine, slot = dev_z(i) if over_z else dev_y(i), z if over_z else y, 6 + 2 * phase + h
                pltpu.make_async_remote_copy(
                    send_h.at[phase, h], recv_h.at[phase, h, mine], ssem.at[slot], rsem.at[slot],
                    device_id=dev, device_id_type=MESH).start()
            dev, mine = (dev_y(i), y) if phase else (dev_z(i), z)
            pltpu.make_async_remote_copy(
                send_d.at[1 + phase], recv_d.at[1 + phase, mine], ssem.at[12 + phase], rsem.at[12 + phase],
                device_id=dev, device_id_type=MESH).start()

        ring(8, send_halves)
        recv_d[1 + phase, y if phase else z] = halves[2]
        for h in range(2):
            recv_h[phase, h, z if (h + phase) % 2 == 0 else y] = halves[h]
        if phase == 1:
            await_bytes(recv_e.at[pl.ds(0, LZ - 1)], rsem.at[4])
            ends_t = recv_e[...].reshape(NT, 128).T
            ends[0] = ends_t[:NS]
            ends[1] = ends_t[NS:]

            def finish(kg, carry):
                for i in range(8):
                    k = kg * 8 + i
                    for ph, m1, m2 in ((0, 3, 2), (1, 5, 4)):
                        c1 = coef[m1, kg, i : i + 1, :]
                        c2_ = coef[m2, kg, i : i + 1, :]
                        high, low = split(snap0[ph * NZ + k] + c1 * ends[0] + c2_ * ends[1])
                        snap[ph * NZ + k, :NS, :] = high
                        snap[ph * NZ + k, NS:, :] = low
                return carry

            lax.fori_loop(0, NZ // 8, finish, 0)
        for h in range(2):
            slot = 6 + 2 * phase + h
            await_bytes(recv_h.at[phase, h, pl.ds(0, 7)], rsem.at[slot])
        await_bytes(recv_d.at[1 + phase, pl.ds(0, 7)], rsem.at[12 + phase])
        halves = [add([recv_h[phase, h, i] for i in range(8)]) for h in range(2)]
        halves.append(add([recv_d[1 + phase, i] for i in range(8)]))
    square = jnp.concatenate(halves[:2], axis=0)
    square = jnp.concatenate([square[:, :NS], square[:, NS:]], axis=0)
    near, side = square[:, :half], square[:, half:]
    flip = near.T
    far = jnp.where(over < down, near, jnp.where(over == down, halves[2][:, :half], flip))
    gram_out[...] = jnp.concatenate([jnp.where(over >= down, near, flip), side, side.T, far], axis=1)

    await_bytes(recv_c.at[pl.ds(0, LZ - 1)], ssem.at[0])
    await_bytes(recv_bu.at[0, pl.ds(0, LZ - 1)], ssem.at[1])
    await_bytes(recv_bu.at[1, pl.ds(0, LZ - 1)], ssem.at[2])
    for part in range(2):
        await_bytes(recv_x.at[part, pl.ds(0, LX - 1)], ssem.at[3 + 8 * part])
    await_bytes(recv_e.at[pl.ds(0, LZ - 1)], ssem.at[4])
    await_bytes(recv_g.at[pl.ds(0, 2 * LX - 1)], ssem.at[5])
    for slot in (10, 12, 13):
        await_bytes(recv_d.at[0, pl.ds(0, 7)], ssem.at[slot])
    for slot in range(6, 10):
        await_bytes(recv_h.at[0, 0, pl.ds(0, 7)], ssem.at[slot])


def reciprocal(d):
    r = pl.reciprocal(d, approx=True)
    return r * (2.0 - d * r)


def rsqrt(d):
    r = lax.rsqrt(d)
    return r * (1.5 - (0.5 * d * r) * r)


def eliminate(gram):
    full = (8, 128)
    rows_i = lax.broadcasted_iota(jnp.int32, full, 0)
    lane_i = lax.broadcasted_iota(jnp.int32, full, 1)
    left = lane_i < NS
    w, on_rows, on_lanes = [], [], jnp.zeros(full, F32)
    for b in range(8):
        part = gram[(b % 4) * 8 : (b % 4) * 8 + 8, :]
        if b >= 4:
            part = pltpu.roll(part, NS, 1)
        diag = jnp.where(lane_i == rows_i + 8 * b, part, 0.0)
        on_rows.append(jnp.broadcast_to(jnp.sum(diag, axis=1, keepdims=True), full))
        on_lanes = on_lanes + diag
        w.append(part)
    on_lanes = jnp.broadcast_to(jnp.sum(on_lanes, axis=0, keepdims=True), full)
    on_lanes = jnp.where(left, on_lanes, pltpu.roll(on_lanes, NS, 1))
    unit = rsqrt(on_lanes)
    undo = jnp.where(left, on_lanes * unit, unit)
    for b in range(8):
        eye = (lane_i == rows_i + (NS + 8 * b)).astype(F32)
        w[b] = jnp.where(left, w[b] * (rsqrt(on_rows[b]) * unit), eye)
    for b in range(8):
        r = [jnp.broadcast_to(w[b][i : i + 1, :], full) for i in range(8)]
        column = lambda u, i: jnp.broadcast_to(u[:, 8 * b + i : 8 * b + i + 1], full)
        d = {(i, j): column(r[i], j) for i in range(8) for j in range(i, 8)}
        cols = {g: [column(w[g], i) for i in range(8)] for g in range(b + 1, 8)}
        done = []
        for i in range(0, 8, 2):
            k = i + 1
            d00, d01, d11 = d[i, i], d[i, k], d[k, k]
            det = d00 * d11 - d01 * d01
            inv = reciprocal(det)
            a00, a01, a11 = d11 * inv, d01 * inv, d00 * inv
            y = {}
            for j in range(i + 2, 8):
                y[j] = (a00 * d[i, j] - a01 * d[k, j], a11 * d[k, j] - a01 * d[i, j])
            x0 = a00 * r[i] - a01 * r[k]
            x1 = a11 * r[k] - a01 * r[i]
            for j in range(i + 2, 8):
                for m in range(j, 8):
                    d[j, m] = d[j, m] - (d[i, j] * y[m][0] + d[k, j] * y[m][1])
                r[j] = r[j] - (d[i, j] * x0 + d[k, j] * x1)
            for g in range(b + 1, 8):
                c = cols[g]
                w[g] = w[g] - (c[i] * x0 + c[k] * x1)
                for j in range(i + 2, 8):
                    c[j] = c[j] - (c[i] * y[j][0] + c[k] * y[j][1])
            done.append(r[i] * rsqrt(d00))
            done.append((d00 * r[k] - d01 * r[i]) * rsqrt(d00 * det))
            if i < 6:
                yield None
        rows = done[0]
        for s in range(1, 8):
            rows = jnp.where(rows_i == s, done[s], rows)
        yield rows * undo


CHUNKS = 8


def basis_kernel(root, gram, snap, basis, factor, out, out_sem):
    per = 2 * NZ // CHUNKS
    half = NS // 2
    stores = []

    def operand(rows, first, depth):
        high, low = split(rows[:, NS : NS + depth] * root)
        return first, depth, jnp.concatenate([high, high, low], axis=1)

    def multiply(i, first, depth, lhs, begin=0, end=per):
        for k in range(i * per + begin, i * per + end):
            high, low = snap[k, :depth, :], snap[k, NS : NS + depth, :]
            res = jnp.dot(lhs, jnp.concatenate([high, low, high], axis=0), preferred_element_type=F32)
            for h in range(2):
                out[h, i, pl.ds(8 * first + k - i * per, half, stride=8), :] = res[:, h * 128 : h * 128 + 128]
        if end < per:
            return
        ph, z0 = divmod(i * per, NZ)
        for h in range(2):
            copy = pltpu.make_async_copy(
                out.at[h, i, pl.ds(8 * first, 8 * half)].reshape(half, 8, 128),
                basis.at[pl.ds(first, half), ph, pl.ds(z0, per), pl.ds(h * 128, 128)],
                out_sem.at[h, i, first // half])
            copy.start()
            stores.append(copy)

    rows, turns, top = [], 0, None
    for block in eliminate(gram):
        if block is not None:
            rows.append(block)
            if len(rows) == 4:
                top = operand(jnp.concatenate(rows, axis=0), 0, half)
                continue
        if top is not None:
            begin = (turns % 2) * (per // 2)
            multiply(turns // 2, *top, begin, begin + per // 2)
            turns += 1
    rows = jnp.concatenate(rows, axis=0)
    bottom = operand(rows[half:], half, NS)
    for i in range(CHUNKS):
        multiply(i, *bottom)
    upper = lax.broadcasted_iota(jnp.int32, (NS, NS), 1) >= lax.broadcasted_iota(jnp.int32, (NS, NS), 0)
    factor[...] = jnp.where(upper, rows[:, :NS] * (1.0 / root), 0.0)
    for copy in stores:
        copy.wait()


def basis_call(total_rows, gram, snap):
    vm, dma = pltpu.VMEM, pltpu.SemaphoreType.DMA
    anywhere = pl.BlockSpec(memory_space=pl.ANY)
    invmem = pl.BlockSpec(memory_space=pltpu.VMEM)
    root = float(total_rows) ** 0.5
    return pl.pallas_call(
        functools.partial(basis_kernel, root),
        out_shape=(
            jax.ShapeDtypeStruct((NS, 2, NZ, NT), F32),
            jax.ShapeDtypeStruct((NS, NS), F32),
        ),
        in_specs=[invmem, invmem],
        out_specs=(anywhere, invmem),
        scratch_shapes=[
            vm((2, CHUNKS, NS * 8, 128), F32),
            dma((2, CHUNKS, 2)),
        ],
        name="basis",
        compiler_params=pltpu.CompilerParams(vmem_limit_bytes=40 << 20),
    )(gram, snap)


def per_device(total_rows, solid_start, inlet, ntu, solid_rate):
    vm, dma = pltpu.VMEM, pltpu.SemaphoreType.DMA
    anywhere = pl.BlockSpec(memory_space=pl.ANY)
    invmem = pl.BlockSpec(memory_space=pltpu.VMEM)
    gram, snap = pl.pallas_call(
        sweep_kernel,
        out_shape=(
            jax.ShapeDtypeStruct((32, 128), F32),
            jax.ShapeDtypeStruct((2 * NZ, 2 * NS, NT), BF16),
        ),
        in_specs=[pl.BlockSpec(memory_space=pltpu.HBM)] * 4,
        out_specs=(invmem, invmem),
        scratch_shapes=[
            vm((NS, NZ, NT), BF16),
            vm((NZ, NT), F32),
            vm((NZ, NT), F32),
            vm((NS, NT), F32),
            vm((2, NZ // 8, NS * 8, 128), F32),
            vm((7, NZ // 8, 8, NT), F32),
            vm((2 * NZ, NS, NT), F32),
            vm((4, NS, NT), F32),
            vm((2, 8, 128), F32),
            vm((2, LZ, SLICE, 128), F32),
            vm((2, SLICE, 128), F32),
            vm((LZ, SLICE, 128), F32),
            vm((16, 128), F32),
            vm((2, 2, 8, 128), F32),
            vm((3, 1, 128), F32),
            vm((LZ, 8, 128), F32),
            vm((2, LZ, SLICE, 128), F32),
            vm((2, LX, SLICE, 128), F32),
            vm((LZ, SLICE, 128), F32),
            vm((2 * LX, 16, 128), F32),
            vm((2, 2, 8, 8, 128), F32),
            vm((3, 8, 1, 128), F32),
            vm((128, 64), F32),
            vm((LZ, SLICE, 128), F32),
            dma((4,)),
            dma((14,)),
            dma((14,)),
        ],
        name="sweep",
        compiler_params=pltpu.CompilerParams(
            collective_id=0, has_side_effects=True, vmem_limit_bytes=40 << 20),
    )(*(pltpu.with_memory_space_constraint(v, pltpu.HBM) for v in (solid_start, inlet, ntu, solid_rate)))
    basis, factor = basis_call(total_rows, gram, snap)
    return basis, factor


def solution(mesh):
    placed = (P(None, "ax", "tr"), P(None, "tr"), P("ax", "tr"), P("ax", "tr"))
    total_rows = 2 * NZ * mesh.shape["ax"] * NT * mesh.shape["tr"]
    return jax.shard_map(
        functools.partial(per_device, total_rows),
        mesh=mesh,
        in_specs=placed,
        out_specs=(P(None, None, "ax", "tr"), P()),
        check_vma=False,
    )
```
